512 devices in a mesh: col: 8 (over z_hi, core), req: 64 (over z_lo, y, x).
Axes of the slice: x: 4, y: 4, z: 16 (z_hi: 4, z_lo: 4; z = z_hi * 4 + z_lo), core: 2. Of those that a mesh axis runs over, the one named last changes fastest.
Arguments:
- event_ids: int32 [131072], P('req'), may hold values from 0 to 32767
- cand_ids: int32 [16384], P('req'), may hold values from 0 to 32767
- cand_request: int32 [16384], P('req'), may hold values from 0 to 63, as said below
- table: bfloat16 [32768, 1024], P(None, 'col'), may hold values from -6 to 6
- w_kv: bfloat16 [1024, 2048], P(None, 'col'), may hold values from -0.1875 to 0.1875
- w_qu: bfloat16 [1024, 2048], P(None, 'col'), may hold values from -0.1875 to 0.1875
- w_out: bfloat16 [1024, 1024], P('col'), may hold values from -0.1875 to 0.1875
Outputs:
- scored: bfloat16 [16384, 1024], P('req', 'col')
The draws below stay inside these ranges and needn't reach their ends.
Inputs may be any that keep to these rules, and one draw needn't show every extreme that they name: `cand_request`: a candidate held on index i of req belongs to one of the 16 requests whose past events lie on indices 16 * (i // 16) to 16 * (i // 16) + 15 of req.
All inputs are finite; a program needn't handle non-finite values.
Results may differ from the reference program's by a relative error of at most 0.0048.
Values may be sent and summed in bfloat16 or wider, within the bound.
A program may use at most 128 MiB of HBM per device.

```python
import math
import jax
import jax.numpy as jnp
from jax import lax

D = 1024
HEADS = 8
DH = 128
GROUP = 16
HIST = 2048
EV_DEV = 2048
CAND_DEV = 256
REQ_GROUP = 16
TABLE_ROWS = 32768
EVENTS = 131072
CANDS = 16384


def draw_event_ids(key, part):
    key = jax.random.fold_in(key, 11)
    group_events = GROUP * EV_DEV
    group_count = EVENTS // group_events
    group_keys = jax.random.split(key, group_count)
    shuffled = jax.vmap(lambda one_key: jax.random.permutation(one_key, TABLE_ROWS))(group_keys)
    return shuffled[:, :group_events].reshape(EVENTS).astype(jnp.int32)


def draw_cand_request(key, part):
    key = jax.random.fold_in(key, 23)
    group_cands = CAND_DEV * GROUP
    position = jnp.arange(CANDS, dtype=jnp.int32)
    group_index = position // group_cands
    within = jax.random.randint(key, (CANDS,), 0, REQ_GROUP, dtype=jnp.int32)
    within = jnp.where(position % group_cands == 0, REQ_GROUP - 1, within)
    within = jnp.where(position % group_cands == 1, 0, within)
    return (group_index * REQ_GROUP + within).astype(jnp.int32)


def set_ends(entries, own_key, low, top_value):
    dims = entries.shape
    index_at = [jax.random.randint(jax.random.fold_in(own_key, axis), (), 0, dims[axis]) for axis in range(len(dims))]
    entries = entries.at[tuple(index_at)].set(low)
    longest = dims.index(max(dims))
    index_at[longest] = (index_at[longest] + 1) % dims[longest]
    return entries.at[tuple(index_at)].set(top_value)


def steps_of(own_key, extent, pieces, low, high):
    def one(dim, blocks):
        steps = jax.random.uniform(jax.random.fold_in(jax.random.fold_in(own_key, 6), dim), (blocks,), jnp.float32, low / len(pieces), high / len(pieces))
        return jnp.repeat(jnp.exp(steps), extent[dim] // blocks).reshape((-1,) + (1,) * (len(extent) - dim - 1))

    gain = one(*pieces[0])
    for cut in pieces[1:]:
        gain = gain * one(*cut)
    return gain


def noise(key, dims, width, most, cuts=(), kind=jnp.bfloat16):
    values = width * jax.random.normal(key, dims, jnp.float32)
    if cuts:
        values = values * steps_of(key, dims, cuts, -0.22, 0.18)
    return jnp.clip(values, -most, most).astype(kind)


def setup_inputs(seed: int = 0) -> dict:
    splits = jax.random.split(jax.random.key(seed), 8)
    return {
        "event_ids": draw_event_ids(jax.random.fold_in(splits[7], 71), 0),
        "cand_ids": set_ends(jax.random.randint(splits[1], (CANDS,), 0, TABLE_ROWS), jax.random.fold_in(splits[1], 1), 0, TABLE_ROWS - 1).astype(jnp.int32),
        "cand_request": draw_cand_request(jax.random.fold_in(splits[7], 71), 0),
        "table": noise(splits[3], (TABLE_ROWS, D), 1.0, 6.0, ((1, 8),)),
        "w_kv": noise(splits[4], (D, 2 * D), D ** -0.5, 0.1875, ((1, 8),)),
        "w_qu": noise(splits[5], (D, 2 * D), D ** -0.5, 0.1875, ((1, 8),)),
        "w_out": noise(splits[6], (D, D), D ** -0.5, 0.1875, ((0, 8),)),
    }


def reference(event_ids, cand_ids, cand_request, table, w_kv, w_qu, w_out):
    hist_rows = jnp.take(table, event_ids, axis=0)
    cand_rows = jnp.take(table, cand_ids, axis=0)
    history = jnp.dot(hist_rows, w_kv, preferred_element_type=jnp.float32).astype(jnp.bfloat16)
    projected = jnp.dot(cand_rows, w_qu, preferred_element_type=jnp.float32).reshape(CANDS, HEADS, 2, DH)
    queries = projected[:, :, 0].astype(jnp.bfloat16)
    gating = jax.nn.silu(projected[:, :, 1])
    group_events = GROUP * EV_DEV
    group_cands = GROUP * CAND_DEV
    group_count = EVENTS // group_events
    block_rows = math.gcd(group_cands, 512)
    history_groups = history.reshape(group_count, group_events, HEADS, 2, DH)
    query_groups = queries.reshape(group_count, group_cands, HEADS, DH)
    request_groups = cand_request.reshape(group_count, group_cands)
    score_scale = 1.0 / math.sqrt(DH)
    offsets = jnp.arange(group_cands // block_rows, dtype=jnp.int32) * block_rows

    def per_group(group_index):
        group_kv = history_groups[group_index]
        group_queries = query_groups[group_index]
        group_requests = request_groups[group_index]
        owner_req = group_index * REQ_GROUP + jnp.arange(group_events, dtype=jnp.int32) // HIST

        def per_head(head_index):
            key_rows = group_kv[:, head_index, 0].astype(jnp.float32)
            value_rows = group_kv[:, head_index, 1].astype(jnp.float32)
            head_queries = group_queries[:, head_index]

            def per_block(offset):
                picked = lax.dynamic_slice_in_dim(head_queries, offset, block_rows, 0).astype(jnp.float32)
                request_ids = lax.dynamic_slice_in_dim(group_requests, offset, block_rows, 0)
                scores = jnp.dot(picked, key_rows.T, precision=lax.Precision.HIGHEST) * score_scale
                allowed = request_ids[:, None] == owner_req[None, :]
                weights = jnp.where(allowed, jax.nn.silu(scores) / HIST, 0.0).astype(jnp.bfloat16)
                weights = lax.optimization_barrier(weights)
                return jnp.dot(weights.astype(jnp.float32), value_rows, precision=lax.Precision.HIGHEST)
            return lax.map(per_block, offsets).reshape(group_cands, DH)
        return lax.map(per_head, jnp.arange(HEADS, dtype=jnp.int32))
    attended = lax.map(per_group, jnp.arange(group_count, dtype=jnp.int32))
    features = jnp.transpose(attended, (0, 2, 1, 3)).reshape(CANDS, D)
    average = lax.optimization_barrier(jnp.sum(features, 1)) / D
    variance = lax.optimization_barrier(jnp.sum(features * features, 1)) / D - average * average
    normed = (features - average[:, None]) * lax.rsqrt(variance[:, None] + 1e-05)
    gated = (normed * gating.reshape(CANDS, D)).astype(jnp.bfloat16)
    result = cand_rows.astype(jnp.float32) + jnp.dot(gated, w_out, preferred_element_type=jnp.float32)
    return result.astype(jnp.bfloat16)
```

```python
import functools
import math

import jax
import jax.numpy as jnp
from jax import lax
from jax.experimental import pallas as pl
from jax.experimental.pallas import tpu as pltpu
from jax.sharding import PartitionSpec as P

D = 1024
DH = 128
GROUP = 16
HIST = 2048
REQ_GROUP = 16
CHUNK = 2048
CAND = 256
PIECES = 8
ROWS = CHUNK // PIECES
LAG = 1
PAIR = 2 * CAND
TILE = 512
MESH = pl.DeviceIdType.MESH
NT = (((1,), (1,)), ((), ()))


def attend_kernel(
    table, w_kv, q_in, msg_in, att_out,
    rows, keys, values, queries, msgs, counts, onehot, parts_out, parts_in, own_part,
    own_sem, ring_send, ring_recv, pair_send, pair_recv,
    q_send, q_recv, m_send, m_recv, p_send, p_recv, local_sem,
):
    col, req = lax.axis_index("col"), lax.axis_index("req")
    z_hi, core = col // 2, col % 2
    z_lo, me = req // 16, req % 16
    z = z_hi * 4 + z_lo

    def at_z(other):
        other = lax.rem(other + 16, 16)
        return (other // 4 * 2 + core, other % 4 * 16 + me)

    above, below = at_z(z + 1), at_z(z - 1)
    sibling = (z_hi * 2 + 1 - core, req)

    def peer(index):
        return (col, z_lo * 16 + index)

    barrier = pltpu.get_barrier_semaphore()
    for other in (above, below, sibling):
        pl.semaphore_signal(barrier, inc=1, device_id=other, device_id_type=MESH)

    def greet(j, carry):
        pl.semaphore_signal(
            barrier, inc=1, device_id=peer(lax.rem(me + j, 16)), device_id_type=MESH
        )
        return carry

    lax.fori_loop(1, 16, greet, 0)

    def place(block, half, p):
        return rows.at[
            pl.ds(pl.multiple_of(p * ROWS, ROWS), ROWS),
            pl.ds(pl.multiple_of((block * 2 + half) * 128, 128), 128),
        ]

    def own_copy(p):
        start = pl.multiple_of(me * CHUNK + p * ROWS, ROWS)
        return pltpu.make_async_copy(
            table.at[pl.ds(start, ROWS), :], place(z_hi, core, p), own_sem.at[p]
        )

    for p in range(PIECES):
        own_copy(p).start()
    q_own = pltpu.make_async_copy(
        q_in, queries.at[pl.ds(pl.multiple_of(me * CAND, CAND), CAND), :], local_sem.at[0]
    )
    m_own = pltpu.make_async_copy(msg_in.at[me], msgs.at[me], local_sem.at[1])
    q_own.start()
    m_own.start()
    pl.semaphore_wait(barrier, 18)

    below_block, above_block = lax.rem(z_hi + 3, 4), lax.rem(z_hi + 1, 4)
    far_block = lax.rem(z_hi + 2, 4)

    def ring(block, p, target, sent, kind):
        return pltpu.make_async_remote_copy(
            src_ref=place(block, core, p),
            dst_ref=place(block, core, p),
            send_sem=ring_send.at[sent, p],
            recv_sem=ring_recv.at[kind, p],
            device_id=target,
            device_id_type=MESH,
        )

    def across(block, p, slot):
        return pltpu.make_async_remote_copy(
            src_ref=place(block, core, p),
            dst_ref=place(block, core, p),
            send_sem=pair_send.at[slot, p],
            recv_sem=pair_recv.at[slot, p],
            device_id=sibling,
            device_id_type=MESH,
        )

    def send_own(p, carry):
        own_copy(p).wait()

        @pl.when(z_lo == 3)
        def _():
            ring(z_hi, p, above, 0, 0).start()

        @pl.when(z_lo == 0)
        def _():
            ring(z_hi, p, below, 1, 1).start()

        across(z_hi, p, 0).start()
        return carry

    lax.fori_loop(0, PIECES, send_own, 0)

    def q_copy(j, slot):
        return pltpu.make_async_remote_copy(
            src_ref=q_in,
            dst_ref=queries.at[pl.ds(pl.multiple_of(slot * CAND, CAND), CAND), :],
            send_sem=q_send.at[j],
            recv_sem=q_recv.at[slot],
            device_id=peer(lax.rem(me + j, 16)),
            device_id_type=MESH,
        )

    def m_copy(j, slot):
        to = lax.rem(me + j, 16)
        return pltpu.make_async_remote_copy(
            src_ref=msg_in.at[to],
            dst_ref=msgs.at[slot],
            send_sem=m_send.at[j],
            recv_sem=m_recv.at[slot],
            device_id=peer(to),
            device_id_type=MESH,
        )

    def spread(j, carry):
        m_copy(j, me).start()
        q_copy(j, me).start()
        return carry

    lax.fori_loop(1, 16, spread, 0)

    def ring_step(t, carry):
        @pl.when(t < PIECES)
        def _():
            p = t
            even = lax.rem(p, 2) == 0
            ring(below_block, p, below, 0, 0).wait_recv()

            @pl.when((z_lo < 3) | even)
            def _():
                @pl.when(z_lo < 3)
                def _():
                    ring(below_block, p, above, 0, 0).start()

                @pl.when(z_lo == 3)
                def _():
                    ring(below_block, p, above, 2, 2).start()

            across(below_block, p, 1).start()
            ring(above_block, p, above, 1, 1).wait_recv()

            @pl.when(z_lo > 0)
            def _():
                ring(above_block, p, below, 1, 1).start()

            @pl.when((z_lo == 0) & jnp.logical_not(even))
            def _():
                ring(above_block, p, below, 2, 2).start()

            across(above_block, p, 2).start()

        @pl.when((t >= LAG) & (t < PIECES + LAG))
        def _():
            p = jnp.maximum(t - LAG, 0)
            even = lax.rem(p, 2) == 0
            ring(far_block, p, above, 2, 2).wait_recv()

            @pl.when(even & (z_lo < 3))
            def _():
                ring(far_block, p, above, 2, 2).start()

            @pl.when(jnp.logical_not(even) & (z_lo > 0))
            def _():
                ring(far_block, p, below, 2, 2).start()

            across(far_block, p, 3).start()

        @pl.when(t >= 2 * LAG)
        def _():
            p = jnp.maximum(t - 2 * LAG, 0)
            across(z_hi, p, 0).wait_recv()
            across(below_block, p, 1).wait_recv()
            across(above_block, p, 2).wait_recv()
            across(far_block, p, 3).wait_recv()
            here = pl.ds(pl.multiple_of(p * ROWS, ROWS), ROWS)
            both = jnp.dot(rows[here, :], w_kv[...], preferred_element_type=jnp.float32)
            both = both.astype(jnp.bfloat16)
            keys[here, :] = both[:, :DH]
            values[here, :] = both[:, DH:]

        return carry

    lax.fori_loop(0, PIECES + 2 * LAG, ring_step, 0)

    q_own.wait()
    m_own.wait()

    def arrived(j, carry):
        src = lax.rem(me + j, 16)
        m_copy(j, src).wait_recv()
        q_copy(j, src).wait_recv()
        return carry

    lax.fori_loop(1, 16, arrived, 0)
    for s in range(8):
        count = msgs[:, s, :]
        high = jnp.floor(count * (1.0 / 256.0))
        low = count - high * 256.0
        counts[:, s * 256 : (s + 1) * 256] = jnp.concatenate(
            [low, high, jnp.zeros((96, 256), jnp.float32)], 0
        ).astype(jnp.bfloat16)

    def mark(src, carry):
        wanted = msgs[src, 8:9, :]
        lane = lax.broadcasted_iota(jnp.int32, (DH, CAND), 0).astype(jnp.float32)
        hot = jnp.where(lane == wanted, 1.0, 0.0) + jnp.where(lane == wanted + 16.0, 256.0, 0.0)
        onehot[pl.ds(pl.multiple_of(src * CAND, CAND), CAND), :] = hot.T.astype(jnp.bfloat16)
        return carry

    lax.fori_loop(0, 16, mark, 0)

    half_scale = 0.5 / math.sqrt(DH)

    def part_copy(to, slot):
        return pltpu.make_async_remote_copy(
            src_ref=parts_out.at[to],
            dst_ref=parts_in.at[slot],
            send_sem=p_send.at[to],
            recv_sem=p_recv.at[slot],
            device_id=peer(to),
            device_id_type=MESH,
        )

    def attend_pair(i, carry):
        pair = lax.rem(me // 2 + 1 + i, 8)
        here = pl.ds(pl.multiple_of(pair * PAIR, PAIR), PAIR)
        picked, hot = queries[here, :], onehot[here, :]
        total = jnp.zeros((PAIR, DH), jnp.float32)
        for r in range(CHUNK // TILE):
            span = slice(r * TILE, (r + 1) * TILE)
            u = lax.dot_general(picked, keys[span, :], NT, preferred_element_type=jnp.float32)
            times = jnp.dot(hot, counts[:, span], preferred_element_type=jnp.float32)
            u = u * half_scale
            weight = ((u + u * jnp.tanh(u)) * times).astype(jnp.bfloat16)
            total += jnp.dot(weight, values[span, :], preferred_element_type=jnp.float32)
        for k in range(2):
            src = pair * 2 + k
            part = total[k * CAND : (k + 1) * CAND]

            @pl.when(src == me)
            def _():
                own_part[...] = part

            @pl.when(src != me)
            def _():
                parts_out[src] = part.astype(jnp.bfloat16)
                part_copy(src, me).start()

        return carry

    lax.fori_loop(0, 8, attend_pair, 0)

    def collect(j, total):
        src = lax.rem(me + j, 16)
        part_copy(src, src).wait_recv()
        own_part[...] += parts_in[src].astype(jnp.float32)
        return total

    lax.fori_loop(1, 16, collect, 0)
    att_out[...] = own_part[...] * (1.0 / HIST)

    def sent_ring(p, carry):
        even = lax.rem(p, 2) == 0

        @pl.when(z_lo == 3)
        def _():
            ring(z_hi, p, above, 0, 0).wait_send()

        @pl.when(z_lo < 3)
        def _():
            ring(below_block, p, above, 0, 0).wait_send()

        @pl.when(z_lo == 0)
        def _():
            ring(z_hi, p, below, 1, 1).wait_send()

        @pl.when(z_lo > 0)
        def _():
            ring(above_block, p, below, 1, 1).wait_send()

        @pl.when(even)
        def _():
            ring(far_block, p, above, 2, 2).wait_send()

        @pl.when(jnp.logical_not(even))
        def _():
            ring(far_block, p, below, 2, 2).wait_send()

        for slot in range(4):
            across(far_block, p, slot).wait_send()
        return carry

    lax.fori_loop(0, PIECES, sent_ring, 0)

    def sent_plane(j, carry):
        m_copy(j, me).wait_send()
        q_copy(j, me).wait_send()
        part_copy(lax.rem(me + j, 16), me).wait_send()
        return carry

    lax.fori_loop(1, 16, sent_plane, 0)


def attended_parts(table, w_kv, queries, msg):
    vmem = pl.BlockSpec(memory_space=pltpu.VMEM)
    dma = pltpu.SemaphoreType.DMA
    return pl.pallas_call(
        attend_kernel,
        out_shape=jax.ShapeDtypeStruct((CAND, DH), jnp.float32),
        in_specs=[pl.BlockSpec(memory_space=pl.ANY), vmem, vmem, vmem],
        out_specs=vmem,
        scratch_shapes=[
            pltpu.VMEM((CHUNK, D), jnp.bfloat16),
            pltpu.VMEM((CHUNK, DH), jnp.bfloat16),
            pltpu.VMEM((CHUNK, DH), jnp.bfloat16),
            pltpu.VMEM((16 * CAND, DH), jnp.bfloat16),
            pltpu.VMEM((16, 16, CAND), jnp.float32),
            pltpu.VMEM((DH, CHUNK), jnp.bfloat16),
            pltpu.VMEM((16 * CAND, DH), jnp.bfloat16),
            pltpu.VMEM((16, CAND, DH), jnp.bfloat16),
            pltpu.VMEM((16, CAND, DH), jnp.bfloat16),
            pltpu.VMEM((CAND, DH), jnp.float32),
            dma((PIECES,)),
            dma((3, PIECES)),
            dma((3, PIECES)),
            dma((4, PIECES)),
            dma((4, PIECES)),
            dma((16,)),
            dma((16,)),
            dma((16,)),
            dma((16,)),
            dma((16,)),
            dma((16,)),
            dma((2,)),
        ],
        compiler_params=pltpu.CompilerParams(
            collective_id=0, has_side_effects=True, vmem_limit_bytes=48 << 20
        ),
        cost_estimate=pl.CostEstimate(
            flops=7 << 30, bytes_accessed=4 << 20, transcendentals=8 << 20
        ),
        name="attend_chunk",
    )(table, w_kv, queries, msg)


def on_device(event_ids, cand_ids, cand_request, table, w_kv, w_qu, w_out):
    cand_slice = jnp.take(table, cand_ids, axis=0)
    projected = jnp.dot(
        lax.all_gather(cand_slice, "col", axis=1, tiled=True),
        w_qu,
        preferred_element_type=jnp.float32,
    )
    queries = projected[:, :DH].astype(jnp.bfloat16)
    gating = jax.nn.silu(projected[:, DH:])
    high = (event_ids[None, :] // 128 == jnp.arange(256, dtype=jnp.int32)[:, None]).astype(
        jnp.bfloat16
    )
    low = (event_ids[None, :] % 128 == jnp.arange(128, dtype=jnp.int32)[:, None]).astype(
        jnp.bfloat16
    )
    times = lax.dot_general(high, low, NT, preferred_element_type=jnp.float32)
    wanted = (cand_request % REQ_GROUP).astype(jnp.float32)
    msg = jnp.concatenate(
        [times.reshape(16, 8, 256), jnp.broadcast_to(wanted[None, None, :], (16, 8, 256))], 1
    )
    features = attended_parts(table, w_kv, queries, msg)
    moments = lax.psum((jnp.sum(features, 1), jnp.sum(features * features, 1)), "col")
    average = moments[0] / D
    variance = moments[1] / D - average * average
    normed = (features - average[:, None]) * lax.rsqrt(variance[:, None] + 1e-05)
    gated = (normed * gating).astype(jnp.bfloat16)
    out_cols = lax.psum_scatter(
        lax.dot_general(w_out, gated, (((0,), (1,)), ((), ())), preferred_element_type=jnp.float32),
        "col",
        scatter_dimension=0,
        tiled=True,
    )
    return (cand_slice.astype(jnp.float32) + out_cols.T).astype(jnp.bfloat16)


def solution(mesh):
    in_specs = (
        P("req"),
        P("req"),
        P("req"),
        P(None, "col"),
        P(None, "col"),
        P(None, "col"),
        P("col", None),
    )
    out_specs = P("req", "col")
    return jax.shard_map(
        on_device, mesh=mesh, in_specs=in_specs, out_specs=out_specs, check_vma=False
    )
```

```python
import functools
import math

import jax
import jax.numpy as jnp
from jax import lax
from jax.experimental import pallas as pl
from jax.experimental.pallas import tpu as pltpu
from jax.sharding import PartitionSpec as P

D = 1024
DH = 128
GROUP = 16
HIST = 2048
REQ_GROUP = 16
CHUNK = 2048
CAND = 256
PIECES = 8
ROWS = CHUNK // PIECES
LAG = 2
CAND_STEP = 6
PAIR = 2 * CAND
TILE = 512
MESH = pl.DeviceIdType.MESH
NT = (((1,), (1,)), ((), ()))


def layer_kernel(
    table, w_kv, w_qu, w_out, cand_in, msg_in, out,
    rows, cands, keys, values, queries, msgs, counts, onehot, gate, parts_out, parts_in, own_part,
    moments, shares, share_out, share_near, share_in,
    own_sem, ring_send, ring_recv, pair_send, pair_recv, c_send, c_recv, cp_send, cp_recv,
    q_send, q_recv, m_send, m_recv, p_send, p_recv, s_send, s_recv, o_send, o_recv,
    x_send, x_recv, local_sem,
):
    col, req = lax.axis_index("col"), lax.axis_index("req")
    z_hi, core = col // 2, col % 2
    z_lo, me = req // 16, req % 16
    z = z_hi * 4 + z_lo

    def at_z(other):
        other = lax.rem(other + 16, 16)
        return (other // 4 * 2 + core, other % 4 * 16 + me)

    above, below = at_z(z + 1), at_z(z - 1)
    sibling = (z_hi * 2 + 1 - core, req)
    mine = pl.ds(pl.multiple_of(me * CAND, CAND), CAND)
    below_block, above_block = lax.rem(z_hi + 3, 4), lax.rem(z_hi + 1, 4)
    far_block = lax.rem(z_hi + 2, 4)

    def peer(index):
        return (col, z_lo * 16 + index)

    def column(block):
        return (block * 2 + core, req)

    def remote(src, dst, sent, arrived, target):
        return pltpu.make_async_remote_copy(
            src_ref=src,
            dst_ref=dst,
            send_sem=sent,
            recv_sem=arrived,
            device_id=target,
            device_id_type=MESH,
        )

    barrier = pltpu.get_barrier_semaphore()
    for other in (above, below):
        pl.semaphore_signal(barrier, inc=1, device_id=other, device_id_type=MESH)

    def greet(j, carry):
        pl.semaphore_signal(
            barrier, inc=1, device_id=peer(lax.rem(me + j, 16)), device_id_type=MESH
        )
        return carry

    lax.fori_loop(1, 16, greet, 0)

    def greet_column(j, carry):
        pl.semaphore_signal(
            barrier, inc=1, device_id=(lax.rem(col + j, 8), req), device_id_type=MESH
        )
        return carry

    lax.fori_loop(1, 8, greet_column, 0)

    def place(block, half, p):
        return rows.at[block * 2 + half, pl.ds(pl.multiple_of(p * ROWS, ROWS), ROWS), :]

    def own_copy(p):
        start = pl.multiple_of(me * CHUNK + p * ROWS, ROWS)
        return pltpu.make_async_copy(
            table.at[pl.ds(start, ROWS), :], place(z_hi, core, p), own_sem.at[p]
        )

    for p in range(PIECES):
        own_copy(p).start()
    m_own = pltpu.make_async_copy(msg_in.at[me], msgs.at[me], local_sem.at[0])
    m_own.start()
    cands[col] = cand_in[...]
    pl.semaphore_wait(barrier, 24)

    def cand_copy(block, target, kind):
        slot = cands.at[block * 2 + core]
        return remote(slot, slot, c_send.at[kind], c_recv.at[kind], column(target))

    cand_copy(z_hi, above_block, 0).start()
    cand_copy(z_hi, below_block, 1).start()
    cand_copy(z_hi, far_block, 2).start()

    def cand_across(block, slot):
        ref = cands.at[block * 2 + core]
        return remote(ref, ref, cp_send.at[slot], cp_recv.at[slot], sibling)

    cand_across(z_hi, 0).start()

    def ring(block, p, target, kind):
        ref = place(block, core, p)
        return remote(ref, ref, ring_send.at[kind, p], ring_recv.at[kind, p], target)

    def across(block, p, slot):
        ref = place(block, core, p)
        return remote(ref, ref, pair_send.at[slot, p], pair_recv.at[slot, p], sibling)

    def send_own(p, carry):
        own_copy(p).wait()

        @pl.when(z_lo == 3)
        def _():
            ring(z_hi, p, above, 0).start()

        @pl.when(z_lo == 0)
        def _():
            ring(z_hi, p, below, 1).start()

        across(z_hi, p, 0).start()
        return carry

    lax.fori_loop(0, PIECES, send_own, 0)

    def m_copy(j, slot):
        to = lax.rem(me + j, 16)
        return remote(msg_in.at[to], msgs.at[slot], m_send.at[j], m_recv.at[slot], peer(to))

    def q_copy(j, slot):
        to = lax.rem(me + j, 16)
        part = queries.at[pl.ds(pl.multiple_of(slot * CAND, CAND), CAND), :]
        return remote(part, part, q_send.at[j], q_recv.at[slot], peer(to))

    def spread_m(j, carry):
        m_copy(j, me).start()
        return carry

    def spread_q(j, carry):
        q_copy(j, me).start()
        return carry

    lax.fori_loop(1, 16, spread_m, 0)

    up_lag, down_lag = LAG * z_lo, LAG * (3 - z_lo)

    def ring_step(t, carry):
        p = t - up_lag

        @pl.when((p >= 0) & (p < PIECES))
        def _():
            ring(below_block, p, below, 0).wait_recv()

            @pl.when(z_lo < 3)
            def _():
                ring(below_block, p, above, 0).start()

            @pl.when((z_lo == 3) & (lax.rem(p, 2) == 0))
            def _():
                ring(below_block, p, above, 2).start()

            across(below_block, p, 1).start()

        p1 = t - down_lag

        @pl.when((p1 >= 0) & (p1 < PIECES))
        def _():
            ring(above_block, p1, above, 1).wait_recv()

            @pl.when(z_lo > 0)
            def _():
                ring(above_block, p1, below, 1).start()

            @pl.when((z_lo == 0) & (lax.rem(p1, 2) == 1))
            def _():
                ring(above_block, p1, below, 2).start()

            across(above_block, p1, 2).start()

        p2 = t - up_lag - 4 * LAG

        @pl.when((p2 >= 0) & (p2 < PIECES) & (lax.rem(p2 + 32, 2) == 0))
        def _():
            ring(far_block, p2, below, 2).wait_recv()

            @pl.when(z_lo < 3)
            def _():
                ring(far_block, p2, above, 2).start()

            across(far_block, p2, 3).start()

        p3 = t - down_lag - 4 * LAG

        @pl.when((p3 >= 0) & (p3 < PIECES) & (lax.rem(p3 + 32, 2) == 1))
        def _():
            ring(far_block, p3, above, 2).wait_recv()

            @pl.when(z_lo > 0)
            def _():
                ring(far_block, p3, below, 2).start()

            across(far_block, p3, 3).start()

        @pl.when(t == CAND_STEP)
        def _():
            cand_copy(below_block, below_block, 0).wait_recv()
            cand_across(below_block, 1).start()
            cand_copy(above_block, above_block, 1).wait_recv()
            cand_across(above_block, 2).start()
            cand_copy(far_block, far_block, 2).wait_recv()
            cand_across(far_block, 3).start()

        @pl.when(t == CAND_STEP + 1)
        def _():
            for slot in range(4):
                cand_across(z_hi, slot).wait_recv()
            joined = jnp.concatenate([cands[k] for k in range(8)], 1)
            both = jnp.dot(joined, w_qu[...], preferred_element_type=jnp.float32)
            queries[mine, :] = both[:, :DH].astype(jnp.bfloat16)
            gate[...] = both[:, DH:]
            lax.fori_loop(1, 16, spread_q, 0)

        p4 = t - 7 * LAG - 1

        @pl.when((p4 >= 0) & (p4 < PIECES))
        def _():
            for slot in range(4):
                across(z_hi, p4, slot).wait_recv()
            here = pl.ds(pl.multiple_of(p4 * ROWS, ROWS), ROWS)
            joined = jnp.concatenate([rows[k, here, :] for k in range(8)], 1)
            both = jnp.dot(joined, w_kv[...], preferred_element_type=jnp.float32)
            both = both.astype(jnp.bfloat16)
            keys[here, :] = both[:, :DH]
            values[here, :] = both[:, DH:]

        return carry

    lax.fori_loop(0, PIECES + 7 * LAG + 1, ring_step, 0)

    m_own.wait()

    def arrived(j, carry):
        src = lax.rem(me + j, 16)
        m_copy(j, src).wait_recv()
        q_copy(j, src).wait_recv()
        return carry

    lax.fori_loop(1, 16, arrived, 0)
    for s in range(8):
        count = msgs[:, s, :]
        high = jnp.floor(count * (1.0 / 256.0))
        low = count - high * 256.0
        counts[:, s * 256 : (s + 1) * 256] = jnp.concatenate(
            [low, high, jnp.zeros((96, 256), jnp.float32)], 0
        ).astype(jnp.bfloat16)

    def mark(src, carry):
        wanted = msgs[src, 8:9, :]
        lane = lax.broadcasted_iota(jnp.int32, (DH, CAND), 0).astype(jnp.float32)
        hot = jnp.where(lane == wanted, 1.0, 0.0) + jnp.where(lane == wanted + 16.0, 256.0, 0.0)
        onehot[pl.ds(pl.multiple_of(src * CAND, CAND), CAND), :] = hot.T.astype(jnp.bfloat16)
        return carry

    lax.fori_loop(0, 16, mark, 0)

    half_scale = 0.5 / math.sqrt(DH)

    def part_copy(to, slot):
        return remote(parts_out.at[to], parts_in.at[slot], p_send.at[to], p_recv.at[slot], peer(to))

    def attend_pair(i, carry):
        pair = lax.rem(me // 2 + 1 + i, 8)
        here = pl.ds(pl.multiple_of(pair * PAIR, PAIR), PAIR)
        picked, hot = queries[here, :], onehot[here, :]
        total = jnp.zeros((PAIR, DH), jnp.float32)
        for r in range(CHUNK // TILE):
            span = slice(r * TILE, (r + 1) * TILE)
            u = lax.dot_general(picked, keys[span, :], NT, preferred_element_type=jnp.float32)
            times = jnp.dot(hot, counts[:, span], preferred_element_type=jnp.float32)
            u = u * half_scale
            weight = ((u + u * jnp.tanh(u)) * times).astype(jnp.bfloat16)
            total += jnp.dot(weight, values[span, :], preferred_element_type=jnp.float32)
        for k in range(2):
            src = pair * 2 + k
            part = total[k * CAND : (k + 1) * CAND]

            @pl.when(src == me)
            def _():
                own_part[...] = part

            @pl.when(src != me)
            def _():
                parts_out[src] = part.astype(jnp.bfloat16)
                part_copy(src, me).start()

        return carry

    lax.fori_loop(0, 8, attend_pair, 0)

    def collect(j, carry):
        src = lax.rem(me + j, 16)
        part_copy(src, src).wait_recv()
        own_part[...] += parts_in[src].astype(jnp.float32)
        return carry

    lax.fori_loop(1, 16, collect, 0)

    attended = (own_part[...] * (1.0 / HIST)).T
    moments[col, 0:1, :] = jnp.sum(attended, axis=0, keepdims=True)
    moments[col, 1:2, :] = jnp.sum(attended * attended, axis=0, keepdims=True)
    moments[col, 2:8, :] = jnp.zeros((6, CAND), jnp.float32)

    def moment_copy(j, slot):
        ref = moments.at[slot]
        return remote(ref, ref, s_send.at[j], s_recv.at[slot], (lax.rem(col + j, 8), req))

    def spread_moments(j, carry):
        moment_copy(j, col).start()
        return carry

    lax.fori_loop(1, 8, spread_moments, 0)
    gate_t = gate[...].T
    gate_t = gate_t / (1.0 + jnp.exp(-gate_t))

    def moments_arrived(j, carry):
        moment_copy(j, lax.rem(col + j, 8)).wait_recv()
        return carry

    lax.fori_loop(1, 8, moments_arrived, 0)
    summed = moments[0]
    for k in range(1, 8):
        summed = summed + moments[k]
    average = summed[0:1, :] * (1.0 / D)
    variance = summed[1:2, :] * (1.0 / D) - average * average
    gated = ((attended - average) * lax.rsqrt(variance + 1e-05) * gate_t).T.astype(jnp.bfloat16)

    product = jnp.dot(gated, w_out[...], preferred_element_type=jnp.float32)
    for k in range(8):
        shares[k] = product[:, k * 128 : (k + 1) * 128]

    def share_across(block):
        return remote(
            shares.at[block * 2 + 1 - core], share_near.at[block], x_send.at[block], x_recv.at[block],
            sibling,
        )

    def share_copy(block, kind):
        return remote(
            share_out.at[kind], share_in.at[kind], o_send.at[kind], o_recv.at[kind], column(block)
        )

    order = ((far_block, 2), (above_block, 0), (below_block, 1))
    for block, _ in order + ((z_hi, 3),):
        share_across(block).start()
    for block, kind in order:
        share_across(block).wait_recv()
        share_out[kind] = (shares[block * 2 + core] + share_near[block]).astype(jnp.bfloat16)
        share_copy(block, kind).start()
    share_across(z_hi).wait_recv()
    own_part[...] = shares[col] + share_near[z_hi] + cand_in[...].astype(jnp.float32)
    for kind in (0, 1, 2):
        share_copy(z_hi, kind).wait_recv()
        own_part[...] += share_in[kind].astype(jnp.float32)
    out[...] = own_part[...].astype(jnp.bfloat16)

    def sent_ring(p, carry):
        for kind in range(3):
            ring(far_block, p, above, kind).wait_send()
        for slot in range(4):
            across(far_block, p, slot).wait_send()
        return carry

    lax.fori_loop(0, PIECES, sent_ring, 0)

    def sent_plane(j, carry):
        m_copy(j, me).wait_send()
        q_copy(j, me).wait_send()
        part_copy(lax.rem(me + j, 16), me).wait_send()
        return carry

    lax.fori_loop(1, 16, sent_plane, 0)

    def sent_moments(j, carry):
        moment_copy(j, col).wait_send()
        return carry

    lax.fori_loop(1, 8, sent_moments, 0)
    for kind in range(3):
        cand_copy(z_hi, far_block, kind).wait_send()
        share_copy(z_hi, kind).wait_send()
    for slot in range(4):
        cand_across(z_hi, slot).wait_send()
        share_across(slot).wait_send()


def layer(table, w_kv, w_qu, w_out, cand_slice, msg):
    vmem = pl.BlockSpec(memory_space=pltpu.VMEM)
    dma = pltpu.SemaphoreType.DMA
    bf16, f32 = jnp.bfloat16, jnp.float32
    return pl.pallas_call(
        layer_kernel,
        out_shape=jax.ShapeDtypeStruct((CAND, DH), bf16),
        in_specs=[pl.BlockSpec(memory_space=pl.ANY)] + [vmem] * 5,
        out_specs=vmem,
        scratch_shapes=[
            pltpu.VMEM((8, CHUNK, 128), bf16),
            pltpu.VMEM((8, CAND, 128), bf16),
            pltpu.VMEM((CHUNK, DH), bf16),
            pltpu.VMEM((CHUNK, DH), bf16),
            pltpu.VMEM((16 * CAND, DH), bf16),
            pltpu.VMEM((16, 16, CAND), f32),
            pltpu.VMEM((DH, CHUNK), bf16),
            pltpu.VMEM((16 * CAND, DH), bf16),
            pltpu.VMEM((CAND, DH), f32),
            pltpu.VMEM((16, CAND, DH), bf16),
            pltpu.VMEM((16, CAND, DH), bf16),
            pltpu.VMEM((CAND, DH), f32),
            pltpu.VMEM((8, 8, CAND), f32),
            pltpu.VMEM((8, CAND, 128), f32),
            pltpu.VMEM((3, CAND, 128), bf16),
            pltpu.VMEM((4, CAND, 128), f32),
            pltpu.VMEM((3, CAND, 128), bf16),
            dma((PIECES,)),
            dma((3, PIECES)),
            dma((3, PIECES)),
            dma((4, PIECES)),
            dma((4, PIECES)),
            dma((3,)),
            dma((3,)),
            dma((4,)),
            dma((4,)),
            dma((16,)),
            dma((16,)),
            dma((16,)),
            dma((16,)),
            dma((16,)),
            dma((16,)),
            dma((8,)),
            dma((8,)),
            dma((3,)),
            dma((3,)),
            dma((4,)),
            dma((4,)),
            dma((1,)),
        ],
        compiler_params=pltpu.CompilerParams(
            collective_id=0, has_side_effects=True, vmem_limit_bytes=48 << 20
        ),
        cost_estimate=pl.CostEstimate(
            flops=8 << 30, bytes_accessed=4 << 20, transcendentals=8 << 20
        ),
        name="layer",
    )(table, w_kv, w_qu, w_out, cand_slice, msg)


def on_device(event_ids, cand_ids, cand_request, table, w_kv, w_qu, w_out):
    cand_slice = jnp.take(table, cand_ids, axis=0)
    high = (event_ids[None, :] // 128 == jnp.arange(256, dtype=jnp.int32)[:, None]).astype(
        jnp.bfloat16
    )
    low = (event_ids[None, :] % 128 == jnp.arange(128, dtype=jnp.int32)[:, None]).astype(
        jnp.bfloat16
    )
    times = lax.dot_general(high, low, NT, preferred_element_type=jnp.float32)
    wanted = (cand_request % REQ_GROUP).astype(jnp.float32)
    msg = jnp.concatenate(
        [times.reshape(16, 8, 256), jnp.broadcast_to(wanted[None, None, :], (16, 8, 256))], 1
    )
    return layer(table, w_kv, w_qu, w_out, cand_slice, msg)


def solution(mesh):
    in_specs = (
        P("req"),
        P("req"),
        P("req"),
        P(None, "col"),
        P(None, "col"),
        P(None, "col"),
        P("col", None),
    )
    out_specs = P("req", "col")
    return jax.shard_map(
        on_device, mesh=mesh, in_specs=in_specs, out_specs=out_specs, check_vma=False
    )
```

```python
import functools
import math

import jax
import jax.numpy as jnp
from jax import lax
from jax.experimental import pallas as pl
from jax.experimental.pallas import tpu as pltpu
from jax.sharding import PartitionSpec as P

D = 1024
DH = 128
GROUP = 16
HIST = 2048
REQ_GROUP = 16
CHUNK = 2048
CAND = 256
PIECES = 8
ROWS = CHUNK // PIECES
LAG = 2
CAND_STEP = 3
FAR_STEP = 5
PAIR = 2 * CAND
TILE = 512
MESH = pl.DeviceIdType.MESH
NT = (((1,), (1,)), ((), ()))


def layer_kernel(
    events, cand_ids, cand_row, wanted_in, table, table_tiles, w_kv_in, w_qu_in, w_out_in, out,
    table_here, w_kv, w_qu, w_out, msg_out, within, rows, cands, keys, values, queries, msgs, counts, onehot, gate, parts_out, parts_in, own_part,
    moments, shares, share_out, share_near, share_in,
    own_sem, ring_send, ring_recv, pair_send, pair_recv, c_send, c_recv, cp_send, cp_recv,
    q_send, q_recv, m_send, m_recv, p_send, p_recv, s_send, s_recv, o_send, o_recv,
    x_send, x_recv, local_sem,
):
    col, req = lax.axis_index("col"), lax.axis_index("req")
    z_hi, core = col // 2, col % 2
    z_lo, me = req // 16, req % 16
    z = z_hi * 4 + z_lo

    def at_z(other):
        other = lax.rem(other + 16, 16)
        return (other // 4 * 2 + core, other % 4 * 16 + me)

    above, below = at_z(z + 1), at_z(z - 1)
    sibling = (z_hi * 2 + 1 - core, req)
    mine = pl.ds(pl.multiple_of(me * CAND, CAND), CAND)
    below_block, above_block = lax.rem(z_hi + 3, 4), lax.rem(z_hi + 1, 4)
    far_block = lax.rem(z_hi + 2, 4)

    def peer(index):
        return (col, z_lo * 16 + index)

    def column(block):
        return (block * 2 + core, req)

    def remote(src, dst, sent, arrived, target):
        return pltpu.make_async_remote_copy(
            src_ref=src,
            dst_ref=dst,
            send_sem=sent,
            recv_sem=arrived,
            device_id=target,
            device_id_type=MESH,
        )

    barrier = pltpu.get_barrier_semaphore()
    for other in (above, below):
        pl.semaphore_signal(barrier, inc=1, device_id=other, device_id_type=MESH)

    def greet(j, carry):
        pl.semaphore_signal(
            barrier, inc=1, device_id=peer(lax.rem(me + j, 16)), device_id_type=MESH
        )
        return carry

    lax.fori_loop(1, 16, greet, 0)

    def greet_column(j, carry):
        pl.semaphore_signal(
            barrier, inc=1, device_id=(lax.rem(col + j, 8), req), device_id_type=MESH
        )
        return carry

    lax.fori_loop(1, 8, greet_column, 0)

    def place(block, half, p):
        return rows.at[block * 2 + half, pl.ds(pl.multiple_of(p * ROWS, ROWS), ROWS), :]

    def own_copy(p):
        start = pl.multiple_of(me * CHUNK + p * ROWS, ROWS)
        return pltpu.make_async_copy(
            table.at[pl.ds(start, ROWS), :], place(z_hi, core, p), own_sem.at[p]
        )

    for p in range(PIECES):
        own_copy(p).start()
    table_copy = pltpu.make_async_copy(table_tiles, table_here, local_sem.at[0])
    kv_copy = pltpu.make_async_copy(w_kv_in, w_kv, local_sem.at[1])
    qu_copy = pltpu.make_async_copy(w_qu_in, w_qu, local_sem.at[2])
    out_copy = pltpu.make_async_copy(w_out_in, w_out, local_sem.at[3])
    for copy in (table_copy, qu_copy, kv_copy, out_copy):
        copy.start()

    place_in = (cand_row[...] & 15).astype(jnp.float32)
    within[...] = jnp.broadcast_to(place_in, (128, CAND)).T
    lane = lax.broadcasted_iota(jnp.int32, (16, 256), 1)
    lane = (lane - 16 * lax.broadcasted_iota(jnp.int32, (16, 256), 0)).astype(jnp.float32)
    table_copy.wait()

    def look_up(g, carry):
        for k in range(4):
            first = pl.multiple_of(g * 64 + k * 16, 16)
            tiles = [table_here[cand_ids[first + i] >> 4] for i in range(16)]
            wide = within[pl.ds(first, 16), :]
            pick = jnp.where(lane == jnp.concatenate([wide, wide], 1), 1.0, 0.0).astype(jnp.bfloat16)
            found = jnp.dot(pick, jnp.concatenate(tiles, 0), preferred_element_type=jnp.float32)
            cands[col, pl.ds(first, 16), :] = found.astype(jnp.bfloat16)
        return carry

    lax.fori_loop(0, 4, look_up, 0)
    pl.semaphore_wait(barrier, 24)

    def cand_copy(block, target, kind):
        slot = cands.at[block * 2 + core]
        return remote(slot, slot, c_send.at[kind], c_recv.at[kind], column(target))

    cand_copy(z_hi, above_block, 0).start()
    cand_copy(z_hi, below_block, 1).start()
    cand_copy(z_hi, far_block, 2).start()

    def cand_across(block, slot):
        ref = cands.at[block * 2 + core]
        return remote(ref, ref, cp_send.at[slot], cp_recv.at[slot], sibling)

    cand_across(z_hi, 0).start()

    def ring(block, p, target, kind):
        ref = place(block, core, p)
        return remote(ref, ref, ring_send.at[kind, p], ring_recv.at[kind, p], target)

    def across(block, p, slot):
        ref = place(block, core, p)
        return remote(ref, ref, pair_send.at[slot, p], pair_recv.at[slot, p], sibling)

    half = PIECES // 2

    def in_turn(i, first):
        return jnp.where(i < half, 2 * i + first, 2 * (i - half) + 1 - first)

    def own_here(p, carry):
        own_copy(p).wait()
        across(z_hi, p, 0).start()
        return carry

    def send_own(i, carry):
        @pl.when(z_lo == 3)
        def _():
            ring(z_hi, in_turn(i, 0), above, 0).start()

        @pl.when(z_lo == 0)
        def _():
            ring(z_hi, in_turn(i, 1), below, 1).start()

        return carry

    lax.fori_loop(0, PIECES, own_here, 0)
    lax.fori_loop(0, PIECES, send_own, 0)

    times = jnp.zeros((256, 128), jnp.float32)
    for k in range(4):
        some = events[:, k * 512 : (k + 1) * 512]
        high = lax.broadcasted_iota(jnp.int32, (256, 512), 0) == some // 128
        low = lax.broadcasted_iota(jnp.int32, (128, 512), 0) == some % 128
        times += lax.dot_general(
            jnp.where(high, 1.0, 0.0).astype(jnp.bfloat16),
            jnp.where(low, 1.0, 0.0).astype(jnp.bfloat16),
            NT,
            preferred_element_type=jnp.float32,
        )
    wanted_here = (wanted_in[...] % REQ_GROUP).astype(jnp.float32)
    for k in range(16):
        msg_out[k, 0:16, :] = times[k * 16 : (k + 1) * 16]
        msg_out[k, 16:18, :] = wanted_here
        msg_out[k, 18:24, :] = jnp.zeros((6, 128), jnp.float32)
    msgs[me] = msg_out[me]

    def m_copy(j, slot):
        to = lax.rem(me + j, 16)
        return remote(msg_out.at[to], msgs.at[slot], m_send.at[j], m_recv.at[slot], peer(to))

    def q_copy(j, slot):
        to = lax.rem(me + j, 16)
        part = queries.at[pl.ds(pl.multiple_of(slot * CAND, CAND), CAND), :]
        return remote(part, part, q_send.at[j], q_recv.at[slot], peer(to))

    def spread_m(j, carry):
        m_copy(j, me).start()
        return carry

    def spread_q(j, carry):
        q_copy(j, me).start()
        return carry

    lax.fori_loop(1, 16, spread_m, 0)

    up_lag, down_lag = LAG * z_lo, LAG * (3 - z_lo)

    def ring_step(t, carry):
        i0 = t - up_lag

        @pl.when((i0 >= 0) & (i0 < PIECES))
        def _():
            p = in_turn(i0, 0)
            ring(below_block, p, below, 0).wait_recv()

            @pl.when(z_lo < 3)
            def _():
                ring(below_block, p, above, 0).start()

            @pl.when((z_lo == 3) & (i0 < half))
            def _():
                ring(below_block, p, above, 2).start()

            across(below_block, p, 1).start()

        i1 = t - down_lag

        @pl.when((i1 >= 0) & (i1 < PIECES))
        def _():
            p = in_turn(i1, 1)
            ring(above_block, p, above, 1).wait_recv()

            @pl.when(z_lo > 0)
            def _():
                ring(above_block, p, below, 1).start()

            @pl.when((z_lo == 0) & (i1 < half))
            def _():
                ring(above_block, p, below, 2).start()

            across(above_block, p, 2).start()

        i2 = t - up_lag - 4 * LAG

        @pl.when((i2 >= 0) & (i2 < half))
        def _():
            p = 2 * i2
            ring(far_block, p, below, 2).wait_recv()

            @pl.when(z_lo < 3)
            def _():
                ring(far_block, p, above, 2).start()

            across(far_block, p, 3).start()

        i3 = t - down_lag - 4 * LAG

        @pl.when((i3 >= 0) & (i3 < half))
        def _():
            p = 2 * i3 + 1
            ring(far_block, p, above, 2).wait_recv()

            @pl.when(z_lo > 0)
            def _():
                ring(far_block, p, below, 2).start()

            across(far_block, p, 3).start()

        @pl.when(t == CAND_STEP)
        def _():
            cand_copy(below_block, below_block, 0).wait_recv()
            cand_across(below_block, 1).start()
            cand_copy(above_block, above_block, 1).wait_recv()
            cand_across(above_block, 2).start()

        @pl.when(t == FAR_STEP)
        def _():
            cand_copy(far_block, far_block, 2).wait_recv()
            cand_across(far_block, 3).start()

        @pl.when(t == FAR_STEP + 1)
        def _():
            for slot in range(4):
                cand_across(z_hi, slot).wait_recv()
            qu_copy.wait()
            joined = jnp.concatenate([cands[k] for k in range(8)], 1)
            both = jnp.dot(joined, w_qu[...], preferred_element_type=jnp.float32)
            queries[mine, :] = both[:, :DH].astype(jnp.bfloat16)
            gate[...] = both[:, DH:]
            lax.fori_loop(1, 16, spread_q, 0)

        i4 = t - 7 * LAG - 1

        @pl.when((i4 >= 0) & (i4 < half))
        def _():
            for slot in range(4):
                across(z_hi, 2 * i4, slot).wait_recv()
                across(z_hi, 2 * i4 + 1, slot).wait_recv()
            here = pl.ds(pl.multiple_of(i4 * 2 * ROWS, 2 * ROWS), 2 * ROWS)
            joined = jnp.concatenate([rows[k, here, :] for k in range(8)], 1)
            both = jnp.dot(joined, w_kv[...], preferred_element_type=jnp.float32)
            both = both.astype(jnp.bfloat16)
            keys[here, :] = both[:, :DH]
            values[here, :] = both[:, DH:]

        return carry

    kv_copy.wait()
    lax.fori_loop(0, PIECES // 2 + 7 * LAG + 1, ring_step, 0)

    def arrived(j, carry):
        src = lax.rem(me + j, 16)
        m_copy(j, src).wait_recv()
        q_copy(j, src).wait_recv()
        return carry

    lax.fori_loop(1, 16, arrived, 0)
    for s in range(16):
        count = msgs[:, s, :]
        high = jnp.floor(count * (1.0 / 256.0))
        low = count - high * 256.0
        counts[:, s * 128 : (s + 1) * 128] = jnp.concatenate(
            [low, high, jnp.zeros((96, 128), jnp.float32)], 0
        ).astype(jnp.bfloat16)

    def mark(src, carry):
        lane = lax.broadcasted_iota(jnp.int32, (DH, 128), 0).astype(jnp.float32)
        for k in range(2):
            wanted = msgs[src, 16 + k : 17 + k, :]
            hot = jnp.where(lane == wanted, 1.0, 0.0) + jnp.where(lane == wanted + 16.0, 256.0, 0.0)
            start = pl.multiple_of(src * CAND + k * 128, 128)
            onehot[pl.ds(start, 128), :] = hot.T.astype(jnp.bfloat16)
        return carry

    lax.fori_loop(0, 16, mark, 0)

    half_scale = 0.5 / math.sqrt(DH)

    def part_copy(to, slot):
        return remote(parts_out.at[to], parts_in.at[slot], p_send.at[to], p_recv.at[slot], peer(to))

    def attend_pair(i, carry):
        pair = lax.rem(me // 2 + 1 + i, 8)
        here = pl.ds(pl.multiple_of(pair * PAIR, PAIR), PAIR)
        picked, hot = queries[here, :], onehot[here, :]
        total = jnp.zeros((PAIR, DH), jnp.float32)
        for r in range(CHUNK // TILE):
            span = slice(r * TILE, (r + 1) * TILE)
            u = lax.dot_general(picked, keys[span, :], NT, preferred_element_type=jnp.float32)
            times = jnp.dot(hot, counts[:, span], preferred_element_type=jnp.float32)
            u = u * half_scale
            weight = ((u + u * jnp.tanh(u)) * times).astype(jnp.bfloat16)
            total += jnp.dot(weight, values[span, :], preferred_element_type=jnp.float32)
        for k in range(2):
            src = pair * 2 + k
            part = total[k * CAND : (k + 1) * CAND]

            @pl.when(src == me)
            def _():
                own_part[...] = part

            @pl.when(src != me)
            def _():
                parts_out[src] = part.astype(jnp.bfloat16)
                part_copy(src, me).start()

        return carry

    lax.fori_loop(0, 8, attend_pair, 0)

    def collect(j, carry):
        src = lax.rem(me + j, 16)
        part_copy(src, src).wait_recv()
        own_part[...] += parts_in[src].astype(jnp.float32)
        return carry

    lax.fori_loop(1, 16, collect, 0)

    attended = (own_part[...] * (1.0 / HIST)).T
    moments[col, 0:1, :] = jnp.sum(attended, axis=0, keepdims=True)
    moments[col, 1:2, :] = jnp.sum(attended * attended, axis=0, keepdims=True)
    moments[col, 2:8, :] = jnp.zeros((6, CAND), jnp.float32)

    def moment_copy(j, slot):
        ref = moments.at[slot]
        return remote(ref, ref, s_send.at[j], s_recv.at[slot], (lax.rem(col + j, 8), req))

    def spread_moments(j, carry):
        moment_copy(j, col).start()
        return carry

    lax.fori_loop(1, 8, spread_moments, 0)
    gate_t = gate[...].T
    gate_t = gate_t / (1.0 + jnp.exp(-gate_t))

    def moments_arrived(j, carry):
        moment_copy(j, lax.rem(col + j, 8)).wait_recv()
        return carry

    lax.fori_loop(1, 8, moments_arrived, 0)
    summed = moments[0]
    for k in range(1, 8):
        summed = summed + moments[k]
    average = summed[0:1, :] * (1.0 / D)
    variance = summed[1:2, :] * (1.0 / D) - average * average
    gated = ((attended - average) * lax.rsqrt(variance + 1e-05) * gate_t).T.astype(jnp.bfloat16)

    out_copy.wait()
    product = jnp.dot(gated, w_out[...], preferred_element_type=jnp.float32)
    for k in range(8):
        shares[k] = product[:, k * 128 : (k + 1) * 128]

    def share_across(block):
        return remote(
            shares.at[block * 2 + 1 - core], share_near.at[block], x_send.at[block], x_recv.at[block],
            sibling,
        )

    def share_copy(block, kind):
        return remote(
            share_out.at[kind], share_in.at[kind], o_send.at[kind], o_recv.at[kind], column(block)
        )

    order = ((far_block, 2), (above_block, 0), (below_block, 1))
    for block, _ in order + ((z_hi, 3),):
        share_across(block).start()
    for block, kind in order:
        share_across(block).wait_recv()
        share_out[kind] = (shares[block * 2 + core] + share_near[block]).astype(jnp.bfloat16)
        share_copy(block, kind).start()
    share_across(z_hi).wait_recv()
    own_part[...] = shares[col] + share_near[z_hi] + cands[col].astype(jnp.float32)
    for kind in (0, 1, 2):
        share_copy(z_hi, kind).wait_recv()
        own_part[...] += share_in[kind].astype(jnp.float32)
    out[...] = own_part[...].astype(jnp.bfloat16)

    def sent_ring(p, carry):
        for kind in range(3):
            ring(far_block, p, above, kind).wait_send()
        for slot in range(4):
            across(far_block, p, slot).wait_send()
        return carry

    lax.fori_loop(0, PIECES, sent_ring, 0)

    def sent_plane(j, carry):
        m_copy(j, me).wait_send()
        q_copy(j, me).wait_send()
        part_copy(lax.rem(me + j, 16), me).wait_send()
        return carry

    lax.fori_loop(1, 16, sent_plane, 0)

    def sent_moments(j, carry):
        moment_copy(j, col).wait_send()
        return carry

    lax.fori_loop(1, 8, sent_moments, 0)
    for kind in range(3):
        cand_copy(z_hi, far_block, kind).wait_send()
        share_copy(z_hi, kind).wait_send()
    for slot in range(4):
        cand_across(z_hi, slot).wait_send()
        share_across(slot).wait_send()


def layer(events, cand_ids, cand_row, wanted, table, w_kv, w_qu, w_out):
    vmem = pl.BlockSpec(memory_space=pltpu.VMEM)
    anywhere = pl.BlockSpec(memory_space=pl.ANY)
    dma = pltpu.SemaphoreType.DMA
    bf16, f32 = jnp.bfloat16, jnp.float32
    return pl.pallas_call(
        layer_kernel,
        out_shape=jax.ShapeDtypeStruct((CAND, DH), bf16),
        in_specs=[vmem, pl.BlockSpec(memory_space=pltpu.SMEM), vmem, vmem] + [anywhere] * 5,
        out_specs=vmem,
        scratch_shapes=[
            pltpu.VMEM((2048, 16, 128), bf16),
            pltpu.VMEM((D, 2 * DH), bf16),
            pltpu.VMEM((D, 2 * DH), bf16),
            pltpu.VMEM((DH, D), bf16),
            pltpu.VMEM((16, 24, 128), f32),
            pltpu.VMEM((CAND, 128), f32),
            pltpu.VMEM((8, CHUNK, 128), bf16),
            pltpu.VMEM((8, CAND, 128), bf16),
            pltpu.VMEM((CHUNK, DH), bf16),
            pltpu.VMEM((CHUNK, DH), bf16),
            pltpu.VMEM((16 * CAND, DH), bf16),
            pltpu.VMEM((16, 24, 128), f32),
            pltpu.VMEM((DH, CHUNK), bf16),
            pltpu.VMEM((16 * CAND, DH), bf16),
            pltpu.VMEM((CAND, DH), f32),
            pltpu.VMEM((16, CAND, DH), bf16),
            pltpu.VMEM((16, CAND, DH), bf16),
            pltpu.VMEM((CAND, DH), f32),
            pltpu.VMEM((8, 8, CAND), f32),
            pltpu.VMEM((8, CAND, 128), f32),
            pltpu.VMEM((3, CAND, 128), bf16),
            pltpu.VMEM((4, CAND, 128), f32),
            pltpu.VMEM((3, CAND, 128), bf16),
            dma((PIECES,)),
            dma((3, PIECES)),
            dma((3, PIECES)),
            dma((4, PIECES)),
            dma((4, PIECES)),
            dma((3,)),
            dma((3,)),
            dma((4,)),
            dma((4,)),
            dma((16,)),
            dma((16,)),
            dma((16,)),
            dma((16,)),
            dma((16,)),
            dma((16,)),
            dma((8,)),
            dma((8,)),
            dma((3,)),
            dma((3,)),
            dma((4,)),
            dma((4,)),
            dma((4,)),
        ],
        compiler_params=pltpu.CompilerParams(
            collective_id=0, has_side_effects=True, vmem_limit_bytes=60 << 20
        ),
        cost_estimate=pl.CostEstimate(
            flops=8 << 30, bytes_accessed=4 << 20, transcendentals=8 << 20
        ),
        name="layer",
    )(events, cand_ids, cand_row, wanted, table, table.reshape(2048, 16, 128), w_kv, w_qu, w_out)


def on_device(event_ids, cand_ids, cand_request, table, w_kv, w_qu, w_out):
    return layer(
        event_ids.reshape(1, HIST),
        cand_ids,
        cand_ids.reshape(1, CAND),
        cand_request.reshape(2, 128),
        table,
        w_kv,
        w_qu,
        w_out,
    )


def solution(mesh):
    in_specs = (
        P("req"),
        P("req"),
        P("req"),
        P(None, "col"),
        P(None, "col"),
        P(None, "col"),
        P("col", None),
    )
    out_specs = P("req", "col")
    return jax.shard_map(
        on_device, mesh=mesh, in_specs=in_specs, out_specs=out_specs, check_vma=False
    )
```

```python
import functools
import math

import jax
import jax.numpy as jnp
from jax import lax
from jax.experimental import pallas as pl
from jax.experimental.pallas import tpu as pltpu
from jax.sharding import PartitionSpec as P

D = 1024
DH = 128
GROUP = 16
HIST = 2048
REQ_GROUP = 16
CHUNK = 2048
CAND = 256
PIECES = 8
ROWS = CHUNK // PIECES
LAG = 2
CAND_STEP = 3
FAR_STEP = 5
PAIR = 2 * CAND
TILE = 512
MESH = pl.DeviceIdType.MESH
NT = (((1,), (1,)), ((), ()))


def layer_kernel(
    events, cand_ids, cand_row, wanted_in, table, table_tiles, w_kv_in, w_qu_in, w_out_in, out,
    table_here, w_kv, w_qu, w_out, msg_out, within, rows, cands, keys, values, queries, msgs, counts, onehot, gate, parts_out, parts_in, own_part,
    moments, shares, share_out, share_near, share_in,
    own_sem, ring_send, ring_recv, pair_send, pair_recv, c_send, c_recv, cp_send, cp_recv,
    q_send, q_recv, m_send, m_recv, p_send, p_recv, s_send, s_recv, o_send, o_recv,
    x_send, x_recv, local_sem,
):
    col, req = lax.axis_index("col"), lax.axis_index("req")
    z_hi, core = col // 2, col % 2
    z_lo, me = req // 16, req % 16
    z = z_hi * 4 + z_lo

    def at_z(other):
        other = lax.rem(other + 16, 16)
        return (other // 4 * 2 + core, other % 4 * 16 + me)

    above, below = at_z(z + 1), at_z(z - 1)
    sibling = (z_hi * 2 + 1 - core, req)
    mine = pl.ds(pl.multiple_of(me * CAND, CAND), CAND)
    below_block, above_block = lax.rem(z_hi + 3, 4), lax.rem(z_hi + 1, 4)
    far_block = lax.rem(z_hi + 2, 4)

    def peer(index):
        return (col, z_lo * 16 + index)

    def column(block):
        return (block * 2 + core, req)

    def remote(src, dst, sent, arrived, target):
        return pltpu.make_async_remote_copy(
            src_ref=src,
            dst_ref=dst,
            send_sem=sent,
            recv_sem=arrived,
            device_id=target,
            device_id_type=MESH,
        )

    def place(block, half, p):
        return rows.at[block * 2 + half, pl.ds(pl.multiple_of(p * ROWS, ROWS), ROWS), :]

    def own_copy(p):
        start = pl.multiple_of(me * CHUNK + p * ROWS, ROWS)
        return pltpu.make_async_copy(
            table.at[pl.ds(start, ROWS), :], place(z_hi, core, p), own_sem.at[p]
        )

    for p in range(PIECES):
        own_copy(p).start()
    table_copy = pltpu.make_async_copy(table_tiles, table_here, local_sem.at[0])
    kv_copy = pltpu.make_async_copy(w_kv_in, w_kv, local_sem.at[1])
    qu_copy = pltpu.make_async_copy(w_qu_in, w_qu, local_sem.at[2])
    out_copy = pltpu.make_async_copy(w_out_in, w_out, local_sem.at[3])
    for copy in (table_copy, qu_copy, kv_copy, out_copy):
        copy.start()

    barrier = pltpu.get_barrier_semaphore()
    def greet_column(j, carry):
        pl.semaphore_signal(
            barrier, inc=1, device_id=(lax.rem(col + j, 8), req), device_id_type=MESH
        )
        return carry

    lax.fori_loop(1, 8, greet_column, 0)

    for other in (above, below):
        pl.semaphore_signal(barrier, inc=1, device_id=other, device_id_type=MESH)

    def greet(j, carry):
        pl.semaphore_signal(
            barrier, inc=1, device_id=peer(lax.rem(me + j, 16)), device_id_type=MESH
        )
        return carry

    lax.fori_loop(1, 16, greet, 0)

    times = jnp.zeros((256, 128), jnp.float32)
    for k in range(4):
        some = events[:, k * 512 : (k + 1) * 512]
        high = lax.broadcasted_iota(jnp.int32, (256, 512), 0) == some // 128
        low = lax.broadcasted_iota(jnp.int32, (128, 512), 0) == some % 128
        times += lax.dot_general(
            jnp.where(high, 1.0, 0.0).astype(jnp.bfloat16),
            jnp.where(low, 1.0, 0.0).astype(jnp.bfloat16),
            NT,
            preferred_element_type=jnp.float32,
        )
    wanted_here = (wanted_in[...] % REQ_GROUP).astype(jnp.float32)
    for k in range(16):
        msg_out[k, 0:16, :] = times[k * 16 : (k + 1) * 16]
        msg_out[k, 16:18, :] = wanted_here
        msg_out[k, 18:24, :] = jnp.zeros((6, 128), jnp.float32)
    msgs[me] = msg_out[me]

    place_in = (cand_row[...] & 15).astype(jnp.float32)
    within[...] = jnp.broadcast_to(place_in, (128, CAND)).T
    lane = lax.broadcasted_iota(jnp.int32, (16, 256), 1)
    lane = (lane - 16 * lax.broadcasted_iota(jnp.int32, (16, 256), 0)).astype(jnp.float32)
    table_copy.wait()

    def look_up(g, carry):
        for k in range(4):
            first = pl.multiple_of(g * 64 + k * 16, 16)
            tiles = [table_here[cand_ids[first + i] >> 4] for i in range(16)]
            wide = within[pl.ds(first, 16), :]
            pick = jnp.where(lane == jnp.concatenate([wide, wide], 1), 1.0, 0.0).astype(jnp.bfloat16)
            found = jnp.dot(pick, jnp.concatenate(tiles, 0), preferred_element_type=jnp.float32)
            cands[col, pl.ds(first, 16), :] = found.astype(jnp.bfloat16)
        return carry

    lax.fori_loop(0, 4, look_up, 0)
    pl.semaphore_wait(barrier, 24)

    def cand_copy(block, target, kind):
        slot = cands.at[block * 2 + core]
        return remote(slot, slot, c_send.at[kind], c_recv.at[kind], column(target))

    cand_copy(z_hi, above_block, 0).start()
    cand_copy(z_hi, below_block, 1).start()
    cand_copy(z_hi, far_block, 2).start()

    def cand_across(block, slot):
        ref = cands.at[block * 2 + core]
        return remote(ref, ref, cp_send.at[slot], cp_recv.at[slot], sibling)

    cand_across(z_hi, 0).start()

    def ring(block, p, target, kind):
        ref = place(block, core, p)
        return remote(ref, ref, ring_send.at[kind, p], ring_recv.at[kind, p], target)

    def across(block, p, slot):
        ref = place(block, core, p)
        return remote(ref, ref, pair_send.at[slot, p], pair_recv.at[slot, p], sibling)

    half = PIECES // 2

    def in_turn(i, first):
        return jnp.where(i < half, 2 * i + first, 2 * (i - half) + 1 - first)

    def own_here(p, carry):
        own_copy(p).wait()
        across(z_hi, p, 0).start()
        return carry

    def send_own(i, carry):
        @pl.when(z_lo == 3)
        def _():
            ring(z_hi, in_turn(i, 0), above, 0).start()

        @pl.when(z_lo == 0)
        def _():
            ring(z_hi, in_turn(i, 1), below, 1).start()

        return carry

    lax.fori_loop(0, PIECES, own_here, 0)
    lax.fori_loop(0, PIECES, send_own, 0)

    def m_copy(j, slot):
        to = lax.rem(me + j, 16)
        return remote(msg_out.at[to], msgs.at[slot], m_send.at[j], m_recv.at[slot], peer(to))

    def q_copy(j, slot):
        to = lax.rem(me + j, 16)
        part = queries.at[pl.ds(pl.multiple_of(slot * CAND, CAND), CAND), :]
        return remote(part, part, q_send.at[j], q_recv.at[slot], peer(to))

    def spread_m(j, carry):
        m_copy(j, me).start()
        return carry

    def spread_q(j, carry):
        q_copy(j, me).start()
        return carry

    lax.fori_loop(1, 16, spread_m, 0)

    def messages(j, carry):
        m_copy(j, lax.rem(me + j, 16)).wait_recv()
        return carry

    up_lag, down_lag = LAG * z_lo, LAG * (3 - z_lo)

    def ring_step(t, carry):
        i0 = t - up_lag

        @pl.when((i0 >= 0) & (i0 < PIECES))
        def _():
            p = in_turn(i0, 0)
            ring(below_block, p, below, 0).wait_recv()

            @pl.when(z_lo < 3)
            def _():
                ring(below_block, p, above, 0).start()

            @pl.when((z_lo == 3) & (i0 < half))
            def _():
                ring(below_block, p, above, 2).start()

            across(below_block, p, 1).start()

        i1 = t - down_lag

        @pl.when((i1 >= 0) & (i1 < PIECES))
        def _():
            p = in_turn(i1, 1)
            ring(above_block, p, above, 1).wait_recv()

            @pl.when(z_lo > 0)
            def _():
                ring(above_block, p, below, 1).start()

            @pl.when((z_lo == 0) & (i1 < half))
            def _():
                ring(above_block, p, below, 2).start()

            across(above_block, p, 2).start()

        i2 = t - up_lag - 4 * LAG

        @pl.when((i2 >= 0) & (i2 < half))
        def _():
            p = 2 * i2
            ring(far_block, p, below, 2).wait_recv()

            @pl.when(z_lo < 3)
            def _():
                ring(far_block, p, above, 2).start()

            across(far_block, p, 3).start()

        i3 = t - down_lag - 4 * LAG

        @pl.when((i3 >= 0) & (i3 < half))
        def _():
            p = 2 * i3 + 1
            ring(far_block, p, above, 2).wait_recv()

            @pl.when(z_lo > 0)
            def _():
                ring(far_block, p, below, 2).start()

            across(far_block, p, 3).start()

        @pl.when(t == CAND_STEP)
        def _():
            cand_copy(below_block, below_block, 0).wait_recv()
            cand_across(below_block, 1).start()
            cand_copy(above_block, above_block, 1).wait_recv()
            cand_across(above_block, 2).start()

        @pl.when(t == FAR_STEP)
        def _():
            cand_copy(far_block, far_block, 2).wait_recv()
            cand_across(far_block, 3).start()

        @pl.when(t == FAR_STEP + 1)
        def _():
            for slot in range(4):
                cand_across(z_hi, slot).wait_recv()
            qu_copy.wait()
            joined = jnp.concatenate([cands[k] for k in range(8)], 1)
            both = jnp.dot(joined, w_qu[...], preferred_element_type=jnp.float32)
            queries[mine, :] = both[:, :DH].astype(jnp.bfloat16)
            gate[...] = both[:, DH:]
            lax.fori_loop(1, 16, spread_q, 0)

        @pl.when(t == 7 * LAG)
        def _():
            lax.fori_loop(1, 16, messages, 0)
            for s in range(16):
                count = msgs[:, s, :]
                high = jnp.floor(count * (1.0 / 256.0))
                low = count - high * 256.0
                counts[:, s * 128 : (s + 1) * 128] = jnp.concatenate(
                    [low, high, jnp.zeros((96, 128), jnp.float32)], 0
                ).astype(jnp.bfloat16)

        i4 = t - 7 * LAG - 1

        @pl.when((i4 >= 0) & (i4 < half))
        def _():
            for slot in range(4):
                across(z_hi, 2 * i4, slot).wait_recv()
                across(z_hi, 2 * i4 + 1, slot).wait_recv()
            here = pl.ds(pl.multiple_of(i4 * 2 * ROWS, 2 * ROWS), 2 * ROWS)
            joined = jnp.concatenate([rows[k, here, :] for k in range(8)], 1)
            both = jnp.dot(joined, w_kv[...], preferred_element_type=jnp.float32)
            both = both.astype(jnp.bfloat16)
            keys[here, :] = both[:, :DH]
            values[here, :] = both[:, DH:]

        return carry

    kv_copy.wait()
    lax.fori_loop(0, PIECES // 2 + 7 * LAG + 1, ring_step, 0)

    def arrived(j, carry):
        q_copy(j, lax.rem(me + j, 16)).wait_recv()
        return carry

    lax.fori_loop(1, 16, arrived, 0)

    def mark(pair):
        lane = lax.broadcasted_iota(jnp.int32, (DH, 128), 0).astype(jnp.float32)
        for k in range(4):
            wanted = msgs[pair * 2 + k // 2, 16 + k % 2 : 17 + k % 2, :]
            hot = jnp.where(lane == wanted, 1.0, 0.0) + jnp.where(lane == wanted + 16.0, 256.0, 0.0)
            start = pl.multiple_of(pair * PAIR + k * 128, 128)
            onehot[pl.ds(start, 128), :] = hot.T.astype(jnp.bfloat16)

    mark(lax.rem(me // 2 + 1, 8))

    half_scale = 0.5 / math.sqrt(DH)

    def part_copy(to, slot):
        return remote(parts_out.at[to], parts_in.at[slot], p_send.at[to], p_recv.at[slot], peer(to))

    def attend_pair(i, carry):
        pair = lax.rem(me // 2 + 1 + i, 8)
        here = pl.ds(pl.multiple_of(pair * PAIR, PAIR), PAIR)
        picked, hot = queries[here, :], onehot[here, :]
        mark(lax.rem(me // 2 + 2 + i, 8))
        total = jnp.zeros((PAIR, DH), jnp.float32)
        for r in range(CHUNK // TILE):
            span = slice(r * TILE, (r + 1) * TILE)
            u = lax.dot_general(picked, keys[span, :], NT, preferred_element_type=jnp.float32)
            times = jnp.dot(hot, counts[:, span], preferred_element_type=jnp.float32)
            u = u * half_scale
            weight = ((u + u * jnp.tanh(u)) * times).astype(jnp.bfloat16)
            total += jnp.dot(weight, values[span, :], preferred_element_type=jnp.float32)
        for k in range(2):
            src = pair * 2 + k
            part = total[k * CAND : (k + 1) * CAND]

            @pl.when(src == me)
            def _():
                own_part[...] = part

            @pl.when(src != me)
            def _():
                parts_out[src] = part.astype(jnp.bfloat16)
                part_copy(src, me).start()

        return carry

    lax.fori_loop(0, 8, attend_pair, 0)

    def collect(d, carry):
        src = lax.rem(me // 2 + 8 - d, 8) * 2
        for k in range(2):
            part_copy(src + k, src + k).wait_recv()
        own_part[...] += parts_in[src].astype(jnp.float32) + parts_in[src + 1].astype(jnp.float32)
        return carry

    lax.fori_loop(1, 8, collect, 0)
    beside = me + 1 - 2 * lax.rem(me, 2)
    part_copy(beside, beside).wait_recv()
    own_part[...] += parts_in[beside].astype(jnp.float32)

    attended = (own_part[...] * (1.0 / HIST)).T
    moments[col, 0:1, :] = jnp.sum(attended, axis=0, keepdims=True)
    moments[col, 1:2, :] = jnp.sum(attended * attended, axis=0, keepdims=True)
    moments[col, 2:8, :] = jnp.zeros((6, CAND), jnp.float32)

    def moment_copy(j, slot):
        ref = moments.at[slot]
        return remote(ref, ref, s_send.at[j], s_recv.at[slot], (lax.rem(col + j, 8), req))

    def spread_moments(j, carry):
        moment_copy(j, col).start()
        return carry

    lax.fori_loop(1, 8, spread_moments, 0)
    gate_t = gate[...].T
    gate_t = gate_t / (1.0 + jnp.exp(-gate_t))

    def moments_arrived(j, carry):
        moment_copy(j, lax.rem(col + j, 8)).wait_recv()
        return carry

    lax.fori_loop(1, 8, moments_arrived, 0)
    summed = moments[0]
    for k in range(1, 8):
        summed = summed + moments[k]
    average = summed[0:1, :] * (1.0 / D)
    variance = summed[1:2, :] * (1.0 / D) - average * average
    gated = ((attended - average) * lax.rsqrt(variance + 1e-05) * gate_t).T.astype(jnp.bfloat16)

    out_copy.wait()
    product = jnp.dot(gated, w_out[...], preferred_element_type=jnp.float32)
    for k in range(8):
        shares[k] = product[:, k * 128 : (k + 1) * 128]

    def share_across(block):
        return remote(
            shares.at[block * 2 + 1 - core], share_near.at[block], x_send.at[block], x_recv.at[block],
            sibling,
        )

    def share_copy(block, kind):
        return remote(
            share_out.at[kind], share_in.at[kind], o_send.at[kind], o_recv.at[kind], column(block)
        )

    order = ((far_block, 2), (above_block, 0), (below_block, 1))
    for block, _ in order + ((z_hi, 3),):
        share_across(block).start()
    for block, kind in order:
        share_across(block).wait_recv()
        share_out[kind] = (shares[block * 2 + core] + share_near[block]).astype(jnp.bfloat16)
        share_copy(block, kind).start()
    share_across(z_hi).wait_recv()
    own_part[...] = shares[col] + share_near[z_hi] + cands[col].astype(jnp.float32)
    for kind in (0, 1, 2):
        share_copy(z_hi, kind).wait_recv()
        own_part[...] += share_in[kind].astype(jnp.float32)
    out[...] = own_part[...].astype(jnp.bfloat16)

    def sent_ring(p, carry):
        for kind in range(3):
            ring(far_block, p, above, kind).wait_send()
        for slot in range(4):
            across(far_block, p, slot).wait_send()
        return carry

    lax.fori_loop(0, PIECES, sent_ring, 0)

    def sent_plane(j, carry):
        m_copy(j, me).wait_send()
        q_copy(j, me).wait_send()
        part_copy(lax.rem(me + j, 16), me).wait_send()
        return carry

    lax.fori_loop(1, 16, sent_plane, 0)

    def sent_moments(j, carry):
        moment_copy(j, col).wait_send()
        return carry

    lax.fori_loop(1, 8, sent_moments, 0)
    for kind in range(3):
        cand_copy(z_hi, far_block, kind).wait_send()
        share_copy(z_hi, kind).wait_send()
    for slot in range(4):
        cand_across(z_hi, slot).wait_send()
        share_across(slot).wait_send()


def layer(events, cand_ids, cand_row, wanted, table, w_kv, w_qu, w_out):
    vmem = pl.BlockSpec(memory_space=pltpu.VMEM)
    anywhere = pl.BlockSpec(memory_space=pl.ANY)
    dma = pltpu.SemaphoreType.DMA
    bf16, f32 = jnp.bfloat16, jnp.float32
    return pl.pallas_call(
        layer_kernel,
        out_shape=jax.ShapeDtypeStruct((CAND, DH), bf16),
        in_specs=[vmem, pl.BlockSpec(memory_space=pltpu.SMEM), vmem, vmem] + [anywhere] * 5,
        out_specs=vmem,
        scratch_shapes=[
            pltpu.VMEM((2048, 16, 128), bf16),
            pltpu.VMEM((D, 2 * DH), bf16),
            pltpu.VMEM((D, 2 * DH), bf16),
            pltpu.VMEM((DH, D), bf16),
            pltpu.VMEM((16, 24, 128), f32),
            pltpu.VMEM((CAND, 128), f32),
            pltpu.VMEM((8, CHUNK, 128), bf16),
            pltpu.VMEM((8, CAND, 128), bf16),
            pltpu.VMEM((CHUNK, DH), bf16),
            pltpu.VMEM((CHUNK, DH), bf16),
            pltpu.VMEM((16 * CAND, DH), bf16),
            pltpu.VMEM((16, 24, 128), f32),
            pltpu.VMEM((DH, CHUNK), bf16),
            pltpu.VMEM((16 * CAND, DH), bf16),
            pltpu.VMEM((CAND, DH), f32),
            pltpu.VMEM((16, CAND, DH), bf16),
            pltpu.VMEM((16, CAND, DH), bf16),
            pltpu.VMEM((CAND, DH), f32),
            pltpu.VMEM((8, 8, CAND), f32),
            pltpu.VMEM((8, CAND, 128), f32),
            pltpu.VMEM((3, CAND, 128), bf16),
            pltpu.VMEM((4, CAND, 128), f32),
            pltpu.VMEM((3, CAND, 128), bf16),
            dma((PIECES,)),
            dma((3, PIECES)),
            dma((3, PIECES)),
            dma((4, PIECES)),
            dma((4, PIECES)),
            dma((3,)),
            dma((3,)),
            dma((4,)),
            dma((4,)),
            dma((16,)),
            dma((16,)),
            dma((16,)),
            dma((16,)),
            dma((16,)),
            dma((16,)),
            dma((8,)),
            dma((8,)),
            dma((3,)),
            dma((3,)),
            dma((4,)),
            dma((4,)),
            dma((4,)),
        ],
        compiler_params=pltpu.CompilerParams(
            collective_id=0, has_side_effects=True, vmem_limit_bytes=60 << 20
        ),
        cost_estimate=pl.CostEstimate(
            flops=8 << 30, bytes_accessed=4 << 20, transcendentals=8 << 20
        ),
        name="layer",
    )(events, cand_ids, cand_row, wanted, table, table.reshape(2048, 16, 128), w_kv, w_qu, w_out)


def on_device(event_ids, cand_ids, cand_request, table, w_kv, w_qu, w_out):
    return layer(
        event_ids.reshape(1, HIST),
        cand_ids,
        cand_ids.reshape(1, CAND),
        cand_request.reshape(2, 128),
        table,
        w_kv,
        w_qu,
        w_out,
    )


def solution(mesh):
    in_specs = (
        P("req"),
        P("req"),
        P("req"),
        P(None, "col"),
        P(None, "col"),
        P(None, "col"),
        P("col", None),
    )
    out_specs = P("req", "col")
    return jax.shard_map(
        on_device, mesh=mesh, in_specs=in_specs, out_specs=out_specs, check_vma=False
    )
```

```python
import functools
import math

import jax
import jax.numpy as jnp
from jax import lax
from jax.experimental import pallas as pl
from jax.experimental.pallas import tpu as pltpu
from jax.sharding import PartitionSpec as P

D = 1024
DH = 128
GROUP = 16
HIST = 2048
REQ_GROUP = 16
CHUNK = 2048
CAND = 256
PIECES = 16
ROWS = CHUNK // PIECES
LAG = 4
CAND_STEP = 6
FAR_STEP = 9
PAIR = 2 * CAND
TILE = 512
MESH = pl.DeviceIdType.MESH
NT = (((1,), (1,)), ((), ()))


def layer_kernel(
    events, cand_ids, cand_row, wanted_in, table, table_tiles, w_kv_in, w_qu_in, w_out_in, out,
    table_here, w_kv, w_qu, w_out, msg_out, within, rows, cands, keys, values, queries, msgs, counts, onehot, gate, parts_out, parts_in, own_part,
    moments, shares, share_out, share_near, share_in,
    own_sem, ring_send, ring_recv, pair_send, pair_recv, c_send, c_recv, cp_send, cp_recv,
    q_send, q_recv, m_send, m_recv, p_send, p_recv, s_send, s_recv, o_send, o_recv,
    x_send, x_recv, local_sem,
):
    col, req = lax.axis_index("col"), lax.axis_index("req")
    z_hi, core = col // 2, col % 2
    z_lo, me = req // 16, req % 16
    z = z_hi * 4 + z_lo

    def at_z(other):
        other = lax.rem(other + 16, 16)
        return (other // 4 * 2 + core, other % 4 * 16 + me)

    above, below = at_z(z + 1), at_z(z - 1)
    sibling = (z_hi * 2 + 1 - core, req)
    mine = pl.ds(pl.multiple_of(me * CAND, CAND), CAND)
    below_block, above_block = lax.rem(z_hi + 3, 4), lax.rem(z_hi + 1, 4)
    far_block = lax.rem(z_hi + 2, 4)

    def peer(index):
        return (col, z_lo * 16 + index)

    def column(block):
        return (block * 2 + core, req)

    def remote(src, dst, sent, arrived, target):
        return pltpu.make_async_remote_copy(
            src_ref=src,
            dst_ref=dst,
            send_sem=sent,
            recv_sem=arrived,
            device_id=target,
            device_id_type=MESH,
        )

    def place(block, half, p):
        return rows.at[block * 2 + half, pl.ds(pl.multiple_of(p * ROWS, ROWS), ROWS), :]

    def own_copy(p):
        start = pl.multiple_of(me * CHUNK + p * ROWS, ROWS)
        return pltpu.make_async_copy(
            table.at[pl.ds(start, ROWS), :], place(z_hi, core, p), own_sem.at[p]
        )

    for p in range(PIECES):
        own_copy(p).start()
    table_copy = pltpu.make_async_copy(table_tiles, table_here, local_sem.at[0])
    kv_copy = pltpu.make_async_copy(w_kv_in, w_kv, local_sem.at[1])
    qu_copy = pltpu.make_async_copy(w_qu_in, w_qu, local_sem.at[2])
    out_copy = pltpu.make_async_copy(w_out_in, w_out, local_sem.at[3])
    for copy in (table_copy, qu_copy, kv_copy, out_copy):
        copy.start()

    barrier = pltpu.get_barrier_semaphore()
    def greet_column(j, carry):
        pl.semaphore_signal(
            barrier, inc=1, device_id=(lax.rem(col + j, 8), req), device_id_type=MESH
        )
        return carry

    lax.fori_loop(1, 8, greet_column, 0)

    for other in (above, below):
        pl.semaphore_signal(barrier, inc=1, device_id=other, device_id_type=MESH)

    def greet(j, carry):
        pl.semaphore_signal(
            barrier, inc=1, device_id=peer(lax.rem(me + j, 16)), device_id_type=MESH
        )
        return carry

    lax.fori_loop(1, 16, greet, 0)

    times = jnp.zeros((256, 128), jnp.float32)
    for k in range(4):
        some = events[:, k * 512 : (k + 1) * 512]
        high = lax.broadcasted_iota(jnp.int32, (256, 512), 0) == some // 128
        low = lax.broadcasted_iota(jnp.int32, (128, 512), 0) == some % 128
        times += lax.dot_general(
            jnp.where(high, 1.0, 0.0).astype(jnp.bfloat16),
            jnp.where(low, 1.0, 0.0).astype(jnp.bfloat16),
            NT,
            preferred_element_type=jnp.float32,
        )
    wanted_here = (wanted_in[...] % REQ_GROUP).astype(jnp.float32)
    for k in range(16):
        msg_out[k, 0:16, :] = times[k * 16 : (k + 1) * 16]
        msg_out[k, 16:18, :] = wanted_here
        msg_out[k, 18:24, :] = jnp.zeros((6, 128), jnp.float32)
    msgs[me] = msg_out[me]

    place_in = (cand_row[...] & 15).astype(jnp.float32)
    within[...] = jnp.broadcast_to(place_in, (128, CAND)).T
    lane = lax.broadcasted_iota(jnp.int32, (16, 256), 1)
    lane = (lane - 16 * lax.broadcasted_iota(jnp.int32, (16, 256), 0)).astype(jnp.float32)
    table_copy.wait()

    def look_up(g, carry):
        for k in range(4):
            first = pl.multiple_of(g * 64 + k * 16, 16)
            tiles = [table_here[cand_ids[first + i] >> 4] for i in range(16)]
            wide = within[pl.ds(first, 16), :]
            pick = jnp.where(lane == jnp.concatenate([wide, wide], 1), 1.0, 0.0).astype(jnp.bfloat16)
            found = jnp.dot(pick, jnp.concatenate(tiles, 0), preferred_element_type=jnp.float32)
            cands[col, pl.ds(first, 16), :] = found.astype(jnp.bfloat16)
        return carry

    lax.fori_loop(0, 4, look_up, 0)
    pl.semaphore_wait(barrier, 24)

    def cand_copy(block, target, kind):
        slot = cands.at[block * 2 + core]
        return remote(slot, slot, c_send.at[kind], c_recv.at[kind], column(target))

    cand_copy(z_hi, above_block, 0).start()
    cand_copy(z_hi, below_block, 1).start()
    cand_copy(z_hi, far_block, 2).start()

    def cand_across(block, slot):
        ref = cands.at[block * 2 + core]
        return remote(ref, ref, cp_send.at[slot], cp_recv.at[slot], sibling)

    cand_across(z_hi, 0).start()

    def ring(block, p, target, kind):
        ref = place(block, core, p)
        return remote(ref, ref, ring_send.at[kind, p], ring_recv.at[kind, p], target)

    def across(block, p, slot):
        ref = place(block, core, p)
        return remote(ref, ref, pair_send.at[slot, p], pair_recv.at[slot, p], sibling)

    half = PIECES // 2

    def in_turn(i, first):
        return jnp.where(i < half, 2 * i + first, 2 * (i - half) + 1 - first)

    def own_here(p, carry):
        own_copy(p).wait()
        across(z_hi, p, 0).start()
        return carry

    def send_own(i, carry):
        @pl.when(z_lo == 3)
        def _():
            ring(z_hi, in_turn(i, 0), above, 0).start()

        @pl.when(z_lo == 0)
        def _():
            ring(z_hi, in_turn(i, 1), below, 1).start()

        return carry

    lax.fori_loop(0, PIECES, own_here, 0)
    lax.fori_loop(0, PIECES, send_own, 0)

    def m_copy(j, slot):
        to = lax.rem(me + j, 16)
        return remote(msg_out.at[to], msgs.at[slot], m_send.at[j], m_recv.at[slot], peer(to))

    def q_copy(j, slot):
        to = lax.rem(me + j, 16)
        part = queries.at[pl.ds(pl.multiple_of(slot * CAND, CAND), CAND), :]
        return remote(part, part, q_send.at[j], q_recv.at[slot], peer(to))

    def spread_m(j, carry):
        m_copy(j, me).start()
        return carry

    def spread_q(j, carry):
        q_copy(j, me).start()
        return carry

    lax.fori_loop(1, 16, spread_m, 0)

    def messages(j, carry):
        m_copy(j, lax.rem(me + j, 16)).wait_recv()
        return carry

    up_lag, down_lag = LAG * z_lo, LAG * (3 - z_lo)

    def ring_step(t, carry):
        i0 = t - up_lag

        @pl.when((i0 >= 0) & (i0 < PIECES))
        def _():
            p = in_turn(i0, 0)
            ring(below_block, p, below, 0).wait_recv()

            @pl.when(z_lo < 3)
            def _():
                ring(below_block, p, above, 0).start()

            @pl.when((z_lo == 3) & (i0 < half))
            def _():
                ring(below_block, p, above, 2).start()

            across(below_block, p, 1).start()

        i1 = t - down_lag

        @pl.when((i1 >= 0) & (i1 < PIECES))
        def _():
            p = in_turn(i1, 1)
            ring(above_block, p, above, 1).wait_recv()

            @pl.when(z_lo > 0)
            def _():
                ring(above_block, p, below, 1).start()

            @pl.when((z_lo == 0) & (i1 < half))
            def _():
                ring(above_block, p, below, 2).start()

            across(above_block, p, 2).start()

        i2 = t - up_lag - 4 * LAG

        @pl.when((i2 >= 0) & (i2 < half))
        def _():
            p = 2 * i2
            ring(far_block, p, below, 2).wait_recv()

            @pl.when(z_lo < 3)
            def _():
                ring(far_block, p, above, 2).start()

            across(far_block, p, 3).start()

        i3 = t - down_lag - 4 * LAG

        @pl.when((i3 >= 0) & (i3 < half))
        def _():
            p = 2 * i3 + 1
            ring(far_block, p, above, 2).wait_recv()

            @pl.when(z_lo > 0)
            def _():
                ring(far_block, p, below, 2).start()

            across(far_block, p, 3).start()

        @pl.when(t == CAND_STEP)
        def _():
            cand_copy(below_block, below_block, 0).wait_recv()
            cand_across(below_block, 1).start()
            cand_copy(above_block, above_block, 1).wait_recv()
            cand_across(above_block, 2).start()

        @pl.when(t == FAR_STEP)
        def _():
            cand_copy(far_block, far_block, 2).wait_recv()
            cand_across(far_block, 3).start()

        @pl.when(t == FAR_STEP + 1)
        def _():
            for slot in range(4):
                cand_across(z_hi, slot).wait_recv()
            qu_copy.wait()
            joined = jnp.concatenate([cands[k] for k in range(8)], 1)
            both = jnp.dot(joined, w_qu[...], preferred_element_type=jnp.float32)
            queries[mine, :] = both[:, :DH].astype(jnp.bfloat16)
            gate[...] = both[:, DH:]
            lax.fori_loop(1, 16, spread_q, 0)

        @pl.when(t == 7 * LAG)
        def _():
            lax.fori_loop(1, 16, messages, 0)
            for s in range(16):
                count = msgs[:, s, :]
                high = jnp.floor(count * (1.0 / 256.0))
                low = count - high * 256.0
                counts[:, s * 128 : (s + 1) * 128] = jnp.concatenate(
                    [low, high, jnp.zeros((96, 128), jnp.float32)], 0
                ).astype(jnp.bfloat16)

        i4 = t - 7 * LAG - 1

        @pl.when((i4 >= 0) & (i4 < half))
        def _():
            for slot in range(4):
                across(z_hi, 2 * i4, slot).wait_recv()
                across(z_hi, 2 * i4 + 1, slot).wait_recv()
            here = pl.ds(pl.multiple_of(i4 * 2 * ROWS, 2 * ROWS), 2 * ROWS)
            joined = jnp.concatenate([rows[k, here, :] for k in range(8)], 1)
            both = jnp.dot(joined, w_kv[...], preferred_element_type=jnp.float32)
            both = both.astype(jnp.bfloat16)
            keys[here, :] = both[:, :DH]
            values[here, :] = both[:, DH:]

        return carry

    kv_copy.wait()
    lax.fori_loop(0, PIECES // 2 + 7 * LAG + 1, ring_step, 0)

    def arrived(j, carry):
        q_copy(j, lax.rem(me + j, 16)).wait_recv()
        return carry

    lax.fori_loop(1, 16, arrived, 0)

    def mark(pair):
        lane = lax.broadcasted_iota(jnp.int32, (DH, 128), 0).astype(jnp.float32)
        for k in range(4):
            wanted = msgs[pair * 2 + k // 2, 16 + k % 2 : 17 + k % 2, :]
            hot = jnp.where(lane == wanted, 1.0, 0.0) + jnp.where(lane == wanted + 16.0, 256.0, 0.0)
            start = pl.multiple_of(pair * PAIR + k * 128, 128)
            onehot[pl.ds(start, 128), :] = hot.T.astype(jnp.bfloat16)

    mark(lax.rem(me // 2 + 1, 8))

    half_scale = 0.5 / math.sqrt(DH)

    def part_copy(to, slot):
        return remote(parts_out.at[to], parts_in.at[slot], p_send.at[to], p_recv.at[slot], peer(to))

    def attend_pair(i, carry):
        pair = lax.rem(me // 2 + 1 + i, 8)
        here = pl.ds(pl.multiple_of(pair * PAIR, PAIR), PAIR)
        picked, hot = queries[here, :], onehot[here, :]
        mark(lax.rem(me // 2 + 2 + i, 8))
        total = jnp.zeros((PAIR, DH), jnp.float32)
        for r in range(CHUNK // TILE):
            span = slice(r * TILE, (r + 1) * TILE)
            u = lax.dot_general(picked, keys[span, :], NT, preferred_element_type=jnp.float32)
            times = jnp.dot(hot, counts[:, span], preferred_element_type=jnp.float32)
            u = u * half_scale
            weight = ((u + u * jnp.tanh(u)) * times).astype(jnp.bfloat16)
            total += jnp.dot(weight, values[span, :], preferred_element_type=jnp.float32)
        for k in range(2):
            src = pair * 2 + k
            part = total[k * CAND : (k + 1) * CAND]

            @pl.when(src == me)
            def _():
                own_part[...] = part

            @pl.when(src != me)
            def _():
                parts_out[src] = part.astype(jnp.bfloat16)
                part_copy(src, me).start()

        return carry

    lax.fori_loop(0, 8, attend_pair, 0)

    def collect(d, carry):
        src = lax.rem(me // 2 + 8 - d, 8) * 2
        for k in range(2):
            part_copy(src + k, src + k).wait_recv()
        own_part[...] += parts_in[src].astype(jnp.float32) + parts_in[src + 1].astype(jnp.float32)
        return carry

    lax.fori_loop(1, 8, collect, 0)
    beside = me + 1 - 2 * lax.rem(me, 2)
    part_copy(beside, beside).wait_recv()
    own_part[...] += parts_in[beside].astype(jnp.float32)

    attended = (own_part[...] * (1.0 / HIST)).T
    moments[col, 0:1, :] = jnp.sum(attended, axis=0, keepdims=True)
    moments[col, 1:2, :] = jnp.sum(attended * attended, axis=0, keepdims=True)
    moments[col, 2:8, :] = jnp.zeros((6, CAND), jnp.float32)

    def moment_copy(j, slot):
        ref = moments.at[slot]
        return remote(ref, ref, s_send.at[j], s_recv.at[slot], (lax.rem(col + j, 8), req))

    def spread_moments(j, carry):
        moment_copy(j, col).start()
        return carry

    lax.fori_loop(1, 8, spread_moments, 0)
    gate_t = gate[...].T
    gate_t = gate_t / (1.0 + jnp.exp(-gate_t))

    def moments_arrived(j, carry):
        moment_copy(j, lax.rem(col + j, 8)).wait_recv()
        return carry

    lax.fori_loop(1, 8, moments_arrived, 0)
    summed = moments[0]
    for k in range(1, 8):
        summed = summed + moments[k]
    average = summed[0:1, :] * (1.0 / D)
    variance = summed[1:2, :] * (1.0 / D) - average * average
    gated = ((attended - average) * lax.rsqrt(variance + 1e-05) * gate_t).T.astype(jnp.bfloat16)

    out_copy.wait()

    def project(slot):
        columns = w_out[:, pl.ds(pl.multiple_of(slot * 128, 128), 128)]
        shares[slot] = jnp.dot(gated, columns, preferred_element_type=jnp.float32)

    def share_across(block):
        return remote(
            shares.at[block * 2 + 1 - core], share_near.at[block], x_send.at[block], x_recv.at[block],
            sibling,
        )

    def share_copy(block, kind):
        return remote(
            share_out.at[kind], share_in.at[kind], o_send.at[kind], o_recv.at[kind], column(block)
        )

    order = ((far_block, 2), (above_block, 0), (below_block, 1))
    for block, _ in order + ((z_hi, 3),):
        project(block * 2 + 1 - core)
        share_across(block).start()
    for block, _ in order + ((z_hi, 3),):
        project(block * 2 + core)
    for block, kind in order:
        share_across(block).wait_recv()
        share_out[kind] = (shares[block * 2 + core] + share_near[block]).astype(jnp.bfloat16)
        share_copy(block, kind).start()
    share_across(z_hi).wait_recv()
    own_part[...] = shares[col] + share_near[z_hi] + cands[col].astype(jnp.float32)
    for kind in (0, 1, 2):
        share_copy(z_hi, kind).wait_recv()
        own_part[...] += share_in[kind].astype(jnp.float32)
    out[...] = own_part[...].astype(jnp.bfloat16)

    def sent_ring(p, carry):
        for kind in range(3):
            ring(far_block, p, above, kind).wait_send()
        for slot in range(4):
            across(far_block, p, slot).wait_send()
        return carry

    lax.fori_loop(0, PIECES, sent_ring, 0)

    def sent_plane(j, carry):
        m_copy(j, me).wait_send()
        q_copy(j, me).wait_send()
        part_copy(lax.rem(me + j, 16), me).wait_send()
        return carry

    lax.fori_loop(1, 16, sent_plane, 0)

    def sent_moments(j, carry):
        moment_copy(j, col).wait_send()
        return carry

    lax.fori_loop(1, 8, sent_moments, 0)
    for kind in range(3):
        cand_copy(z_hi, far_block, kind).wait_send()
        share_copy(z_hi, kind).wait_send()
    for slot in range(4):
        cand_across(z_hi, slot).wait_send()
        share_across(slot).wait_send()


def layer(events, cand_ids, cand_row, wanted, table, w_kv, w_qu, w_out):
    vmem = pl.BlockSpec(memory_space=pltpu.VMEM)
    anywhere = pl.BlockSpec(memory_space=pl.ANY)
    dma = pltpu.SemaphoreType.DMA
    bf16, f32 = jnp.bfloat16, jnp.float32
    return pl.pallas_call(
        layer_kernel,
        out_shape=jax.ShapeDtypeStruct((CAND, DH), bf16),
        in_specs=[vmem, pl.BlockSpec(memory_space=pltpu.SMEM), vmem, vmem] + [anywhere] * 5,
        out_specs=vmem,
        scratch_shapes=[
            pltpu.VMEM((2048, 16, 128), bf16),
            pltpu.VMEM((D, 2 * DH), bf16),
            pltpu.VMEM((D, 2 * DH), bf16),
            pltpu.VMEM((DH, D), bf16),
            pltpu.VMEM((16, 24, 128), f32),
            pltpu.VMEM((CAND, 128), f32),
            pltpu.VMEM((8, CHUNK, 128), bf16),
            pltpu.VMEM((8, CAND, 128), bf16),
            pltpu.VMEM((CHUNK, DH), bf16),
            pltpu.VMEM((CHUNK, DH), bf16),
            pltpu.VMEM((16 * CAND, DH), bf16),
            pltpu.VMEM((16, 24, 128), f32),
            pltpu.VMEM((DH, CHUNK), bf16),
            pltpu.VMEM((16 * CAND, DH), bf16),
            pltpu.VMEM((CAND, DH), f32),
            pltpu.VMEM((16, CAND, DH), bf16),
            pltpu.VMEM((16, CAND, DH), bf16),
            pltpu.VMEM((CAND, DH), f32),
            pltpu.VMEM((8, 8, CAND), f32),
            pltpu.VMEM((8, CAND, 128), f32),
            pltpu.VMEM((3, CAND, 128), bf16),
            pltpu.VMEM((4, CAND, 128), f32),
            pltpu.VMEM((3, CAND, 128), bf16),
            dma((PIECES,)),
            dma((3, PIECES)),
            dma((3, PIECES)),
            dma((4, PIECES)),
            dma((4, PIECES)),
            dma((3,)),
            dma((3,)),
            dma((4,)),
            dma((4,)),
            dma((16,)),
            dma((16,)),
            dma((16,)),
            dma((16,)),
            dma((16,)),
            dma((16,)),
            dma((8,)),
            dma((8,)),
            dma((3,)),
            dma((3,)),
            dma((4,)),
            dma((4,)),
            dma((4,)),
        ],
        compiler_params=pltpu.CompilerParams(
            collective_id=0, has_side_effects=True, vmem_limit_bytes=60 << 20
        ),
        cost_estimate=pl.CostEstimate(
            flops=8 << 30, bytes_accessed=4 << 20, transcendentals=8 << 20
        ),
        name="layer",
    )(events, cand_ids, cand_row, wanted, table, table.reshape(2048, 16, 128), w_kv, w_qu, w_out)


def on_device(event_ids, cand_ids, cand_request, table, w_kv, w_qu, w_out):
    return layer(
        event_ids.reshape(1, HIST),
        cand_ids,
        cand_ids.reshape(1, CAND),
        cand_request.reshape(2, 128),
        table,
        w_kv,
        w_qu,
        w_out,
    )


def solution(mesh):
    in_specs = (
        P("req"),
        P("req"),
        P("req"),
        P(None, "col"),
        P(None, "col"),
        P(None, "col"),
        P("col", None),
    )
    out_specs = P("req", "col")
    return jax.shard_map(
        on_device, mesh=mesh, in_specs=in_specs, out_specs=out_specs, check_vma=False
    )
```
